512 devices in a mesh: rep: 16 (over z_hi, x, core), fsdp: 32 (over y, z_lo).
Axes of the slice: x: 4, y: 8, z: 8 (z_hi: 2, z_lo: 4; z = z_hi * 4 + z_lo), core: 2. Of those that a mesh axis runs over, the one named last changes fastest.
Arguments:
- activations: bfloat16 [65536, 8192], P(('rep', 'fsdp')), may hold values from -24 to 24
- queries: bfloat16 [65536, 4096], P(('rep', 'fsdp')), may hold values from -5 to 5
- keys: bfloat16 [65536, 512], P(('rep', 'fsdp')), may hold values from -5 to 5
- values: bfloat16 [65536, 512], P(('rep', 'fsdp')), may hold values from -6 to 6
- out_grad: bfloat16 [65536, 4096], P(('rep', 'fsdp')), may hold values from -3 to 3
- positions: int32 [65536], P(('rep', 'fsdp')), may hold values from 0 to 127, as said below
- shard_table: int32 [16, 32, 2], P('rep', 'fsdp'), may hold values from 0 to 8192, as said below
Outputs:
- key_grad: bfloat16 [65536, 512], P(('rep', 'fsdp'))
- weight_grad: bfloat16 [16, 32, 320, 512], P('rep', 'fsdp')
The draws below stay inside these ranges and needn't reach their ends.
Inputs may be any that keep to these rules, and one draw needn't show every extreme that they name: shard_table[r, f] = (offset, length): device f of group r holds rows offset to offset + length - 1; in every group these runs follow f in order and cover all 8192 rows once. In all groups but one, offset = f * 256 and length = 256; in the remaining group every run lies within 128 rows of rows f * 256 to (f + 1) * 256 - 1, and some length is 320. Within each device's 128 tokens, positions count up by one from 0 at each document's first token; a device's first token has position 0.
All inputs are finite; a program needn't handle non-finite values.
Results may differ from the reference program's by a relative error of at most 0.0064.
Values may be sent and summed in bfloat16 or wider, within the bound.
A program may use at most 64 MiB of HBM per device.

```python
import math
import jax
import jax.numpy as jnp
from jax import lax

D = 8192
HEAD = 128
GROUP = 8
KV_HEADS = 4
TOK = 128
SLOT = 320
TOKENS = 65536
N_REP = 16
N_FSDP = 32


def document_positions(base_key):
    key_docs = jax.random.fold_in(base_key, 7)
    devices = N_REP * N_FSDP
    rolled = jax.random.randint(key_docs, (devices, TOK), 0, 24)
    index = jnp.arange(TOK, dtype=jnp.int32)
    single_document = (jnp.arange(devices) % 4 == 0)[:, None]
    starts = (rolled == 0) & jnp.logical_not(single_document) | (index == 0)[None, :]
    start_marks = jnp.where(starts, index[None, :], 0)
    latest_start = lax.cummax(start_marks, axis=1)
    return (index[None, :] - latest_start).reshape(devices * TOK).astype(jnp.int32)


def draw_positions(key, part):
    return document_positions(key)


def draw_queries(key, part):
    key = jax.random.fold_in(key, 3)
    return jnp.clip(jax.random.normal(key, (TOKENS, KV_HEADS * GROUP * HEAD), jnp.float32), -5.0, 5.0).astype(jnp.bfloat16)


def draw_keys(key, part):
    key = jax.random.fold_in(key, 5)
    return jnp.clip(jax.random.normal(key, (TOKENS, KV_HEADS * HEAD), jnp.float32), -5.0, 5.0).astype(jnp.bfloat16)


def draw_shard_table(key, part):
    key = jax.random.fold_in(key, 11)
    key_lost, key_force, key_group = jax.random.split(key, 3)
    stride = D // N_FSDP
    candidates = (N_FSDP - 5) // 5 + 1
    places = 2 + 5 * jnp.arange(candidates, dtype=jnp.int32)
    picked = jax.random.randint(key_lost, (candidates,), 0, 2)
    forced = jax.random.randint(key_force, (), 0, candidates)
    picked = jnp.maximum(picked, (jnp.arange(candidates) == forced).astype(jnp.int32))
    missing = jnp.zeros((N_FSDP + 4,), jnp.int32).at[places + 2].set(picked)
    beside_all = missing[0:N_FSDP] + missing[1:N_FSDP + 1] + missing[3:N_FSDP + 3] + missing[4:N_FSDP + 4]
    lengths = stride - stride * missing[2:N_FSDP + 2] + stride // 4 * beside_all
    offsets = jnp.cumsum(lengths) - lengths
    ragged = jnp.stack([offsets, lengths], axis=1)
    evenly = jnp.stack([jnp.arange(N_FSDP, dtype=jnp.int32) * stride, jnp.full((N_FSDP,), stride, jnp.int32)], axis=1)
    broken = jax.random.randint(key_group, (), 0, N_REP)
    chosen = (jnp.arange(N_REP) == broken)[:, None, None]
    return jnp.where(chosen, ragged[None], evenly[None]).astype(jnp.int32)


def strengthened(drawn, stream_key, source, target, parts, factor):
    owner, partner = [(jnp.arange(drawn.shape[dim]) // (drawn.shape[dim] // parts)).reshape([-1 if axis == dim else 1 for axis in range(drawn.ndim)]) for dim in (source, target)]
    chosen = jax.random.permutation(stream_key, parts)[partner]
    strong = (owner == chosen) | (owner == (partner + parts // 2) % parts)
    return jnp.where(strong, factor * drawn, drawn)


def block_scale(own_key, shape, cuts, low, high):
    def one(dim, parts):
        draws = jax.random.uniform(jax.random.fold_in(jax.random.fold_in(own_key, 6), dim), (parts,), jnp.float32, low / len(cuts), high / len(cuts))
        return jnp.repeat(jnp.exp(draws), shape[dim] // parts).reshape((-1,) + (1,) * (len(shape) - dim - 1))

    level = one(*cuts[0])
    for cut in cuts[1:]:
        level = level * one(*cut)
    return level


def gaussian(key, extent, deviation, bound, pieces=(), kind=jnp.bfloat16):
    drawn = jax.random.normal(key, extent, jnp.float32) * deviation
    if len(pieces) > 0:
        drawn = block_scale(key, extent, pieces, -0.22, 0.18) * drawn
    return jnp.clip(drawn, min=-bound, max=bound).astype(kind)


def noise_with(own_key, extent, scale, limit, cuts, heavy, kind=jnp.bfloat16):
    values = scale * jax.random.normal(own_key, extent, jnp.float32)
    if cuts:
        values = values * block_scale(own_key, extent, cuts, -0.22, 0.18)
    return jnp.clip(strengthened(values, jax.random.fold_in(own_key, 3), *heavy), -limit, limit).astype(kind)


def setup_inputs(seed: int = 0) -> dict:
    seeds = jax.random.split(jax.random.key(seed), 8)
    return {
        "activations": noise_with(seeds[0], (TOKENS, D), 1.0, 24.0, ((0, 512),), (0, 1, 512, 6.0)),
        "queries": draw_queries(jax.random.fold_in(seeds[7], 71), 0),
        "keys": draw_keys(jax.random.fold_in(seeds[7], 71), 0),
        "values": gaussian(seeds[3], (TOKENS, KV_HEADS * HEAD), 1.0, 6.0, ((0, 512),)),
        "out_grad": gaussian(seeds[4], (TOKENS, KV_HEADS * GROUP * HEAD), 0.5, 3.0, ((0, 512),)),
        "positions": draw_positions(jax.random.fold_in(seeds[7], 71), 0),
        "shard_table": draw_shard_table(jax.random.fold_in(seeds[7], 71), 0),
    }


def block_backward(operands):
    queries, keys, values, out_grad, positions = operands
    rows_here = queries.shape[0]
    factor = 1.0 / math.sqrt(HEAD)
    query_heads = queries.astype(jnp.float32).reshape(rows_here, KV_HEADS, GROUP, HEAD)
    key_heads = keys.astype(jnp.float32).reshape(rows_here, KV_HEADS, HEAD)
    value_heads = values.astype(jnp.float32).reshape(rows_here, KV_HEADS, HEAD)
    grad_heads = out_grad.astype(jnp.float32).reshape(rows_here, KV_HEADS, GROUP, HEAD)
    scores = jnp.einsum('tkgd,ukd->kgtu', query_heads, key_heads) * factor
    query_index = jnp.arange(rows_here, dtype=jnp.int32)[:, None]
    key_index = jnp.arange(rows_here, dtype=jnp.int32)[None, :]
    allowed = (key_index <= query_index) & (key_index >= query_index - positions[:, None])
    scores = jnp.where(allowed, scores, -1e+30)
    largest = lax.optimization_barrier(jnp.max(scores, axis=-1, keepdims=True))
    raised = jnp.exp(scores - largest)
    attention = raised / lax.optimization_barrier(jnp.sum(raised, axis=-1, keepdims=True))
    attention_low = attention.astype(jnp.bfloat16).astype(jnp.float32)
    attended = jnp.einsum('kgtu,ukd->tkgd', attention_low, value_heads)
    row_dots = lax.optimization_barrier(jnp.sum(grad_heads * attended, axis=-1))
    prob_grads = jnp.einsum('tkgd,ukd->kgtu', grad_heads, value_heads)
    score_grads = (attention * (prob_grads - jnp.transpose(row_dots, (1, 2, 0))[..., None])).astype(jnp.bfloat16)
    value_grad = jnp.einsum('kgtu,tkgd->ukd', attention_low, grad_heads).astype(jnp.bfloat16)
    key_grad = (jnp.einsum('kgtu,tkgd->ukd', score_grads.astype(jnp.float32), query_heads) * factor).astype(jnp.bfloat16)
    return (value_grad.reshape(rows_here, KV_HEADS * HEAD), key_grad.reshape(rows_here, KV_HEADS * HEAD))

def reference(activations, queries, keys, values, out_grad, positions, shard_table):
    devices = N_REP * N_FSDP
    blocks = (queries.reshape(devices, TOK, KV_HEADS * GROUP * HEAD), keys.reshape(devices, TOK, KV_HEADS * HEAD), values.reshape(devices, TOK, KV_HEADS * HEAD), out_grad.reshape(devices, TOK, KV_HEADS * GROUP * HEAD), positions.reshape(devices, TOK))
    value_grad, key_grad = lax.map(block_backward, blocks)
    value_grad = value_grad.reshape(TOKENS, KV_HEADS * HEAD)
    key_grad = key_grad.reshape(TOKENS, KV_HEADS * HEAD)
    full_grad = lax.dot_general(activations, value_grad, (((0,), (0,)), ((), ())), preferred_element_type=jnp.float32) * (1.0 / math.sqrt(TOKENS))
    offsets = shard_table[:, :, 0]
    lengths = shard_table[:, :, 1]
    within = jnp.arange(SLOT, dtype=jnp.int32)
    picked = jnp.clip(offsets[:, :, None] + within[None, None, :], 0, D - 1).astype(jnp.int32)
    gathered = jnp.take(full_grad, picked.reshape(N_REP * N_FSDP * SLOT), axis=0).reshape(N_REP, N_FSDP, SLOT, KV_HEADS * HEAD)
    inside = within[None, None, :] < lengths[:, :, None]
    weight_grad = jnp.where(inside[..., None], gathered, 0.0).astype(jnp.bfloat16)
    return (key_grad, weight_grad)
```

```python
import math

import jax
import jax.numpy as jnp
from jax import lax
from jax.experimental import pallas as pl
from jax.experimental.pallas import tpu as pltpu
from jax.sharding import PartitionSpec as P

HEAD = 128
GROUP = 8
KV_HEADS = 4
NX, NY, NZ, NZL, CORES = 4, 8, 8, 4, 2
RING = 8
BLOCK = 128
HALF = 64
BF16, F32 = jnp.bfloat16, jnp.float32
MESH = pl.DeviceIdType.MESH
FLOWS = (("y", 1, 0), ("y", -1, 1), ("z", 1, 2), ("z", -1, 3))


def device(x, y, z, c):
    zh, zl = z // NZL, lax.rem(z, NZL)
    return ((zh * NX + x) * CORES + c, y * NZL + zl)


def wrap(value, size):
    return lax.rem(value + 2 * size, size)


def nt_dot(a, b):
    return lax.dot_general(a, b, (((1,), (1,)), ((), ())), preferred_element_type=F32)


def kernel(
    q_ref, k_ref, v_ref, g_ref, pos_ref, acts_ref,
    key_ref, win_ref,
    acts_buf, vgt_buf, probs_buf, ring_send, ring_recv,
    zx_send, zx_recv, yx_send, yx_recv, x_send, x_recv, window,
    local_sem, acts_sems, vg_sems, ring_ssem, ring_rsem,
    zx_ssem, zx_rsem, yx_ssem, yx_rsem, x_ssem, x_rsem,
    gather_ssem, gather_rsem, spread_ssem, spread_rsem,
):
    rep, fsdp = lax.axis_index("rep"), lax.axis_index("fsdp")
    c = lax.rem(rep, CORES)
    x = lax.rem(rep // CORES, NX)
    zh = rep // (CORES * NX)
    y, zl = fsdp // NZL, lax.rem(fsdp, NZL)
    z = zh * NZL + zl
    sibling = device(x, y, z, 1 - c)
    f_count = NY * NZL
    far = lax.rem(fsdp + f_count - 1 + 2 * c, f_count)
    far_other = lax.rem(fsdp + f_count + 1 - 2 * c, f_count)

    partners = [sibling]
    partners += [device(x, wrap(y + i, NY), z, c) for i in range(1, NY)]
    partners += [device(x, y, wrap(z + i, NZ), c) for i in range(1, NZ)]
    partners += [device(wrap(x + i, NX), y, z, c) for i in range(1, NX)]
    partners += [device(wrap(x + i, NX), y, wrap(z + NZL, NZ), c) for i in range(1, NX)]
    for other in (far, far_other):
        partners += [(rep, other), (rep + 1 - 2 * c, other)]
    barrier = pltpu.get_barrier_semaphore()
    for partner in partners:
        pl.semaphore_signal(barrier, inc=1, device_id=partner, device_id_type=MESH)

    def local_acts(f):
        return pltpu.make_async_copy(
            acts_ref.at[:, pl.ds(pl.multiple_of(2 * BLOCK * f + BLOCK * c, BLOCK), BLOCK)],
            acts_buf.at[f, pl.ds(0, BLOCK)],
            local_sem.at[0],
        )

    def send_acts(f):
        return pltpu.make_async_remote_copy(
            src_ref=acts_ref.at[
                :, pl.ds(pl.multiple_of(2 * BLOCK * f + BLOCK * (1 - c), BLOCK), BLOCK)
            ],
            dst_ref=acts_buf.at[f, pl.ds(BLOCK, BLOCK)],
            send_sem=acts_sems.at[0],
            recv_sem=acts_sems.at[1],
            device_id=sibling,
            device_id_type=MESH,
        )

    @pl.loop(0, f_count)
    def _(f):
        local_acts(f).start()

    factor = 1.0 / math.sqrt(HEAD)
    key_index = lax.broadcasted_iota(jnp.int32, (BLOCK, BLOCK), 0)
    query_index = lax.broadcasted_iota(jnp.int32, (BLOCK, BLOCK), 1)
    allowed = (key_index <= query_index) & (key_index >= query_index - pos_ref[...])
    allowed = jnp.concatenate((allowed, allowed), axis=1)

    def stacked(ref, first):
        return jnp.concatenate(
            [ref[:, pl.ds(pl.multiple_of(first + i * HEAD, HEAD), HEAD)] for i in range(2)], axis=0
        )

    def values_of(g):
        keys = k_ref[:, pl.ds(pl.multiple_of(g * HEAD, HEAD), HEAD)]
        total = jnp.zeros((BLOCK, HEAD), F32)
        for pair in range(GROUP // 2):
            first = g * GROUP * HEAD + pair * 2 * HEAD
            scores = nt_dot(keys, stacked(q_ref, first)) * factor
            scores = jnp.where(allowed, scores, -1e30)
            raised = jnp.exp(scores - jnp.max(scores, axis=0, keepdims=True))
            probs = raised / jnp.sum(raised, axis=0, keepdims=True)
            probs_buf[g * (GROUP // 2) + pair] = probs
            total += jnp.dot(
                probs.astype(BF16), stacked(g_ref, first), preferred_element_type=F32
            )
        vgt_buf[pl.ds(pl.multiple_of(g * HEAD, HEAD), HEAD), pl.ds(0, BLOCK)] = total.T.astype(BF16)

    @pl.loop(0, 2)
    def _(g):
        values_of(g)

    pl.semaphore_wait(barrier, len(partners))

    @pl.loop(0, f_count)
    def _(f):
        send_acts(f).start()

    @pl.loop(2, KV_HEADS)
    def _(g):
        values_of(g)

    vg_copy = pltpu.make_async_remote_copy(
        src_ref=vgt_buf.at[:, pl.ds(0, BLOCK)],
        dst_ref=vgt_buf.at[:, pl.ds(BLOCK, BLOCK)],
        send_sem=vg_sems.at[0],
        recv_sem=vg_sems.at[1],
        device_id=sibling,
        device_id_type=MESH,
    )
    vg_copy.start()
    own_half = acts_buf.at[:, pl.ds(0, BLOCK)]
    far_half = acts_buf.at[:, pl.ds(BLOCK, BLOCK)]
    pltpu.make_async_copy(own_half, own_half, local_sem.at[0]).wait()
    pltpu.make_async_copy(far_half, far_half, acts_sems.at[1]).wait()
    vg_copy.wait_recv()

    def place(axis):
        return y if axis == "y" else z

    def ring_copy(flow, step, sub):
        axis, way, _ = FLOWS[flow]
        if axis == "y":
            target = device(x, wrap(y + way, NY), z, c)
        else:
            target = device(x, y, wrap(z + way, NZ), c)
        return pltpu.make_async_remote_copy(
            src_ref=ring_send.at[flow, step, sub],
            dst_ref=ring_recv.at[flow, step, sub],
            send_sem=ring_ssem.at[flow, step, sub],
            recv_sem=ring_rsem.at[flow, step, sub],
            device_id=target,
            device_id_type=MESH,
        )

    def partial(flow, step, sub):
        axis, way, g = FLOWS[flow]
        chunk = wrap(place(axis) - way * (1 + step), RING)
        if axis == "y":
            columns = g * HEAD + sub * HALF
            blocks = [acts_buf[chunk * NZL + i] for i in range(4)]
        else:
            columns = pl.multiple_of(g * HEAD + (chunk // NZL) * HALF, HALF)
            blocks = [acts_buf[(4 * sub + i) * NZL + lax.rem(chunk, NZL)] for i in range(4)]
        return jnp.dot(
            vgt_buf[pl.ds(columns, HALF), :],
            jnp.concatenate(blocks, axis=1),
            preferred_element_type=F32,
        )

    def ring_step(step, first):
        for sub in range(2):
            for flow in range(4):
                total = partial(flow, step, sub)
                if not first:
                    ring_copy(flow, step - 1, sub).wait_recv()
                    total += ring_recv[flow, step - 1, sub].astype(F32)
                ring_send[flow, step, sub] = total.astype(BF16)
                ring_copy(flow, step, sub).start()

    ring_step(0, True)

    @pl.loop(0, KV_HEADS)
    def _(g):
        columns = pl.ds(pl.multiple_of(g * HEAD, HEAD), HEAD)
        values = v_ref[:, columns]
        total = jnp.zeros((BLOCK, HEAD), F32)
        for pair in range(GROUP // 2):
            first = g * GROUP * HEAD + pair * 2 * HEAD
            prob_grads = nt_dot(values, stacked(g_ref, first))
            probs = probs_buf[g * (GROUP // 2) + pair]
            row_dots = jnp.sum(
                probs.astype(BF16).astype(F32) * prob_grads, axis=0, keepdims=True
            )
            score_grads = (probs * (prob_grads - row_dots)).astype(BF16)
            total += jnp.dot(score_grads, stacked(q_ref, first), preferred_element_type=F32)
        key_ref[:, columns] = (total * factor).astype(BF16)

    @pl.loop(1, RING - 1)
    def _(step):
        ring_step(step, False)

    last = RING - 1
    for sub in range(2):
        for flow in range(4):
            total = partial(flow, last, sub)
            ring_copy(flow, last - 1, sub).wait_recv()
            total = (total + ring_recv[flow, last - 1, sub].astype(F32)).astype(BF16)
            for i in range(4):
                piece = total[:, i * BLOCK : (i + 1) * BLOCK]
                if FLOWS[flow][0] == "y":
                    zx_send[sub * NZL + i, flow] = piece
                else:
                    yx_send[4 * sub + i, flow - 2] = piece

    def zx_copy(to, slot, i):
        return pltpu.make_async_remote_copy(
            src_ref=zx_send.at[to], dst_ref=zx_recv.at[slot],
            send_sem=zx_ssem.at[i], recv_sem=zx_rsem.at[slot],
            device_id=device(x, y, to, c), device_id_type=MESH,
        )

    def yx_copy(to, slot, i):
        return pltpu.make_async_remote_copy(
            src_ref=yx_send.at[to], dst_ref=yx_recv.at[slot],
            send_sem=yx_ssem.at[i], recv_sem=yx_rsem.at[slot],
            device_id=device(x, to, z, c), device_id_type=MESH,
        )

    for i in range(1, RING):
        zx_copy(wrap(z + i, NZ), z, i).start()
        yx_copy(wrap(y + i, NY), y, i).start()
    zx_recv[z] = zx_send[z]
    yx_recv[y] = yx_send[y]
    for i in range(1, RING):
        zx_copy(wrap(z + i, NZ), wrap(z - i, NZ), i).wait_recv()
        yx_copy(wrap(y + i, NY), wrap(y - i, NY), i).wait_recv()
    zx_total = zx_recv[0].astype(F32)
    yx_total = yx_recv[0].astype(F32)
    for i in range(1, RING):
        zx_total += zx_recv[i].astype(F32)
        yx_total += yx_recv[i].astype(F32)
    x_send[0:2] = zx_total.astype(BF16)
    x_send[2:4] = yx_total.astype(BF16)

    def x_copy(to, slot, i):
        return pltpu.make_async_remote_copy(
            src_ref=x_send.at[to], dst_ref=x_recv.at[slot],
            send_sem=x_ssem.at[i], recv_sem=x_rsem.at[slot],
            device_id=device(to, y, z, c), device_id_type=MESH,
        )

    for i in range(1, NX):
        x_copy(wrap(x + i, NX), x, i).start()
    x_recv[x] = x_send[x]
    for i in range(1, NX):
        x_copy(wrap(x + i, NX), wrap(x - i, NX), i).wait_recv()
    final = x_recv[0].astype(F32)
    for i in range(1, NX):
        final += x_recv[i].astype(F32)
    final = final * (1.0 / math.sqrt(BLOCK * f_count * NX * CORES * (NZ // NZL)))

    def gather_copy(from_x, from_zh, to_x, to_zh, i, slot):
        rows = pl.ds(pl.multiple_of(from_x * HEAD + from_zh * HALF, HALF), HALF)
        return pltpu.make_async_remote_copy(
            src_ref=window.at[1 + c, rows], dst_ref=window.at[1 + c, rows],
            send_sem=gather_ssem.at[i], recv_sem=gather_rsem.at[slot],
            device_id=device(to_x, y, to_zh * NZL + zl, c), device_id_type=MESH,
        )

    own_rows = pl.ds(pl.multiple_of(x * HEAD + zh * HALF, HALF), HALF)
    window[1 + c, own_rows] = final.astype(BF16)
    moves = [(i, j) for j in (1, 0) for i in range(NX) if i or j]
    for n, (i, j) in enumerate(moves):
        to_x, to_zh = wrap(x + i, NX), wrap(zh + j, 2)
        gather_copy(x, zh, to_x, to_zh, n, zh * NX + x).start()
    for n, (i, j) in enumerate(moves):
        from_x, from_zh = wrap(x - i, NX), wrap(zh - j, 2)
        gather_copy(from_x, from_zh, x, zh, n, from_zh * NX + from_x).wait_recv()

    def spread_copy(block, slot, target):
        return pltpu.make_async_remote_copy(
            src_ref=window.at[1 + c], dst_ref=window.at[block],
            send_sem=spread_ssem.at[slot], recv_sem=spread_rsem.at[slot],
            device_id=target, device_id_type=MESH,
        )

    outer = 3 * (1 - c)

    def outer_copy(n, target):
        return pltpu.make_async_remote_copy(
            src_ref=window.at[1 + c], dst_ref=window.at[outer],
            send_sem=spread_ssem.at[1 + n], recv_sem=spread_rsem.at[1 + c],
            device_id=target, device_id_type=MESH,
        )

    outer_copy(0, (rep, far)).start()
    outer_copy(1, (rep + 1 - 2 * c, far)).start()
    spread_copy(1 + c, 0, sibling).start()

    def put(block):
        win_ref[block * BLOCK : (block + 1) * BLOCK, :] = window[block].astype(F32).T.astype(BF16)

    win_ref[4 * BLOCK :, :] = jnp.zeros((BLOCK, KV_HEADS * HEAD), BF16)
    pltpu.make_async_copy(window.at[2 - c], window.at[2 - c], spread_rsem.at[0]).wait()
    put(1)
    put(2)
    for n, block in ((0, 3), (1, 0)):
        pltpu.make_async_copy(window.at[block], window.at[block], spread_rsem.at[1 + n]).wait()
        put(block)

    pltpu.make_async_copy(far_half, far_half, acts_sems.at[0]).wait()
    vg_copy.wait_send()

    @pl.loop(0, RING - 1)
    def _(step):
        for flow in range(4):
            for sub in range(2):
                ring_copy(flow, step, sub).wait_send()

    for i in range(1, RING):
        zx_copy(wrap(z + i, NZ), z, i).wait_send()
        yx_copy(wrap(y + i, NY), y, i).wait_send()
    for i in range(1, NX):
        x_copy(wrap(x + i, NX), x, i).wait_send()
    for n, (i, j) in enumerate(moves):
        gather_copy(x, zh, wrap(x + i, NX), wrap(zh + j, 2), n, zh * NX + x).wait_send()
    outer_copy(0, (rep, far)).wait_send()
    outer_copy(1, (rep + 1 - 2 * c, far)).wait_send()
    spread_copy(1 + c, 0, sibling).wait_send()


def backward(activations, queries, keys, values, out_grad, positions):
    width = KV_HEADS * HEAD
    vmem = pl.BlockSpec(memory_space=pltpu.VMEM)
    dma = pltpu.SemaphoreType.DMA
    ring = (4, RING - 1, 2)
    return pl.pallas_call(
        kernel,
        out_shape=(
            jax.ShapeDtypeStruct((BLOCK, width), BF16),
            jax.ShapeDtypeStruct((5 * BLOCK, width), BF16),
        ),
        in_specs=[vmem] * 5 + [pl.BlockSpec(memory_space=pl.ANY)],
        out_specs=(vmem, vmem),
        scratch_shapes=[
            pltpu.VMEM((NY * NZL, 2 * BLOCK, BLOCK), BF16),
            pltpu.VMEM((width, 2 * BLOCK), BF16),
            pltpu.VMEM((KV_HEADS * GROUP // 2, BLOCK, 2 * BLOCK), F32),
            pltpu.VMEM(ring + (HALF, 4 * BLOCK), BF16),
            pltpu.VMEM(ring + (HALF, 4 * BLOCK), BF16),
            pltpu.VMEM((NZ, 2, HALF, BLOCK), BF16),
            pltpu.VMEM((NZ, 2, HALF, BLOCK), BF16),
            pltpu.VMEM((NY, 2, HALF, BLOCK), BF16),
            pltpu.VMEM((NY, 2, HALF, BLOCK), BF16),
            pltpu.VMEM((NX, HALF, BLOCK), BF16),
            pltpu.VMEM((NX, HALF, BLOCK), BF16),
            pltpu.VMEM((4, width, BLOCK), BF16),
            dma((1,)), dma((2,)), dma((2,)), dma(ring), dma(ring),
            dma((RING,)), dma((RING,)), dma((RING,)), dma((RING,)), dma((NX,)), dma((NX,)),
            dma((RING,)), dma((RING,)), dma((3,)), dma((3,)),
        ],
        compiler_params=pltpu.CompilerParams(
            collective_id=0, has_side_effects=True, vmem_limit_bytes=48 * 1024 * 1024
        ),
        cost_estimate=pl.CostEstimate(
            flops=2 * 10**9, bytes_accessed=6 * 2**20, transcendentals=2**19
        ),
    )(queries, keys, values, out_grad, positions.reshape(1, BLOCK), activations)


def shards(activations, queries, keys, values, out_grad, positions, shard_table):
    key_grad, window = backward(activations, queries, keys, values, out_grad, positions)
    stride = activations.shape[1] // lax.axis_size("fsdp")
    margin = stride // 2
    slot_rows = stride + stride // 4
    device_index = lax.axis_index("fsdp")
    offset = shard_table[0, 0, 0]
    length = shard_table[0, 0, 1]
    first_row = offset - (device_index * stride - margin)
    picked = lax.dynamic_slice_in_dim(window, first_row, slot_rows, 0)
    inside = jnp.arange(slot_rows, dtype=jnp.int32) < length
    slot_grad = jnp.where(inside[:, None], picked, jnp.zeros((), BF16))
    return (key_grad, slot_grad.reshape(1, 1, slot_rows, slot_grad.shape[1]))


def solution(mesh):
    return jax.shard_map(
        shards,
        mesh=mesh,
        in_specs=(
            P(("rep", "fsdp"), None),
            P(("rep", "fsdp"), None),
            P(("rep", "fsdp"), None),
            P(("rep", "fsdp"), None),
            P(("rep", "fsdp"), None),
            P(("rep", "fsdp")),
            P("rep", "fsdp", None),
        ),
        out_specs=(P(("rep", "fsdp"), None), P("rep", "fsdp", None, None)),
        check_vma=False,
    )
```

```python
import math

import jax
import jax.numpy as jnp
from jax import lax
from jax.experimental import pallas as pl
from jax.experimental.pallas import tpu as pltpu
from jax.sharding import PartitionSpec as P

HEAD = 128
GROUP = 8
KV_HEADS = 4
NX, NY, NZ, NZL, CORES = 4, 8, 8, 4, 2
RING = 8
BLOCK = 128
HALF = 64
BF16, F32 = jnp.bfloat16, jnp.float32
MESH = pl.DeviceIdType.MESH
FLOWS = (("y", 1, 0), ("y", -1, 1), ("z", 1, 2), ("z", -1, 3))


def device(x, y, z, c):
    zh, zl = z // NZL, lax.rem(z, NZL)
    return ((zh * NX + x) * CORES + c, y * NZL + zl)


def wrap(value, size):
    return lax.rem(value + 2 * size, size)


def nt_dot(a, b):
    return lax.dot_general(a, b, (((1,), (1,)), ((), ())), preferred_element_type=F32)


def kernel(
    table_ref, pos_ref, q_hbm, k_hbm, v_hbm, g_hbm, acts_ref,
    key_ref, slot_ref,
    q_ref, k_ref, v_ref, g_ref, acts_buf, vgt_buf, probs_buf, ring_send, ring_recv,
    zx_send, zx_recv, yx_send, yx_recv, x_send, x_recv, window,
    load_sems, local_sem, acts_sems, vg_sems, ring_ssem, ring_rsem,
    zx_ssem, zx_rsem, yx_ssem, yx_rsem, x_ssem, x_rsem,
    gather_ssem, gather_rsem, spread_ssem, spread_rsem,
):
    rep, fsdp = lax.axis_index("rep"), lax.axis_index("fsdp")
    c = lax.rem(rep, CORES)
    x = lax.rem(rep // CORES, NX)
    zh = rep // (CORES * NX)
    y, zl = fsdp // NZL, lax.rem(fsdp, NZL)
    z = zh * NZL + zl
    sibling = device(x, y, z, 1 - c)
    f_count = NY * NZL
    far = lax.rem(fsdp + f_count - 1 + 2 * c, f_count)
    far_other = lax.rem(fsdp + f_count + 1 - 2 * c, f_count)

    heads = KV_HEADS * HEAD
    span = GROUP * HEAD

    def load(n, source, target, first, size):
        part = pl.ds(first, size)
        return pltpu.make_async_copy(source.at[:, part], target.at[:, part], load_sems.at[n])

    load_keys = load(0, k_hbm, k_ref, 0, heads)
    load_values = load(1, v_hbm, v_ref, 0, heads)
    load_queries = [load(2 + g, q_hbm, q_ref, g * span, span) for g in range(KV_HEADS)]
    load_grads = [load(6 + g, g_hbm, g_ref, g * span, span) for g in range(KV_HEADS)]
    load_keys.start()
    for g in range(KV_HEADS):
        load_queries[g].start()
        load_grads[g].start()
    load_values.start()

    partners = [sibling]
    partners += [device(x, wrap(y + i, NY), z, c) for i in range(1, NY)]
    partners += [device(x, y, wrap(z + i, NZ), c) for i in range(1, NZ)]
    partners += [device(wrap(x + i, NX), y, z, c) for i in range(1, NX)]
    partners += [device(wrap(x + i, NX), y, wrap(z + NZL, NZ), c) for i in range(1, NX)]
    for other in (far, far_other):
        partners += [(rep, other), (rep + 1 - 2 * c, other)]
    barrier = pltpu.get_barrier_semaphore()
    for partner in partners:
        pl.semaphore_signal(barrier, inc=1, device_id=partner, device_id_type=MESH)

    def local_acts(f):
        return pltpu.make_async_copy(
            acts_ref.at[:, pl.ds(pl.multiple_of(2 * BLOCK * f + BLOCK * c, BLOCK), BLOCK)],
            acts_buf.at[f, pl.ds(0, BLOCK)],
            local_sem.at[0],
        )

    def send_acts(f):
        return pltpu.make_async_remote_copy(
            src_ref=acts_ref.at[
                :, pl.ds(pl.multiple_of(2 * BLOCK * f + BLOCK * (1 - c), BLOCK), BLOCK)
            ],
            dst_ref=acts_buf.at[f, pl.ds(BLOCK, BLOCK)],
            send_sem=acts_sems.at[0],
            recv_sem=acts_sems.at[1],
            device_id=sibling,
            device_id_type=MESH,
        )

    @pl.loop(0, f_count)
    def _(f):
        local_acts(f).start()

    factor = 1.0 / math.sqrt(HEAD)
    key_index = lax.broadcasted_iota(jnp.int32, (BLOCK, BLOCK), 0)
    query_index = lax.broadcasted_iota(jnp.int32, (BLOCK, BLOCK), 1)
    allowed = (key_index <= query_index) & (key_index >= query_index - pos_ref[...])
    allowed = jnp.concatenate((allowed, allowed), axis=1)

    def stacked(ref, first):
        return jnp.concatenate(
            [ref[:, pl.ds(pl.multiple_of(first + i * HEAD, HEAD), HEAD)] for i in range(2)], axis=0
        )

    def values_of(g):
        keys = k_ref[:, pl.ds(pl.multiple_of(g * HEAD, HEAD), HEAD)]
        total = jnp.zeros((BLOCK, HEAD), F32)
        for pair in range(GROUP // 2):
            first = g * GROUP * HEAD + pair * 2 * HEAD
            scores = nt_dot(keys, stacked(q_ref, first)) * factor
            scores = jnp.where(allowed, scores, -1e30)
            raised = jnp.exp(scores - jnp.max(scores, axis=0, keepdims=True))
            probs = raised / jnp.sum(raised, axis=0, keepdims=True)
            probs_buf[g * (GROUP // 2) + pair] = probs
            total += jnp.dot(
                probs.astype(BF16), stacked(g_ref, first), preferred_element_type=F32
            )
        vgt_buf[pl.ds(pl.multiple_of(g * HEAD, HEAD), HEAD), pl.ds(0, BLOCK)] = total.T.astype(BF16)

    load_keys.wait()
    for g in range(2):
        load_queries[g].wait()
        load_grads[g].wait()

    @pl.loop(0, 2)
    def _(g):
        values_of(g)

    pl.semaphore_wait(barrier, len(partners))

    @pl.loop(0, f_count)
    def _(f):
        send_acts(f).start()

    for g in range(2, KV_HEADS):
        load_queries[g].wait()
        load_grads[g].wait()

    @pl.loop(2, KV_HEADS)
    def _(g):
        values_of(g)

    vg_copy = pltpu.make_async_remote_copy(
        src_ref=vgt_buf.at[:, pl.ds(0, BLOCK)],
        dst_ref=vgt_buf.at[:, pl.ds(BLOCK, BLOCK)],
        send_sem=vg_sems.at[0],
        recv_sem=vg_sems.at[1],
        device_id=sibling,
        device_id_type=MESH,
    )
    vg_copy.start()
    own_half = acts_buf.at[:, pl.ds(0, BLOCK)]
    far_half = acts_buf.at[:, pl.ds(BLOCK, BLOCK)]
    pltpu.make_async_copy(own_half, own_half, local_sem.at[0]).wait()
    pltpu.make_async_copy(far_half, far_half, acts_sems.at[1]).wait()
    vg_copy.wait_recv()

    def place(axis):
        return y if axis == "y" else z

    def ring_copy(flow, step, sub):
        axis, way, _ = FLOWS[flow]
        if axis == "y":
            target = device(x, wrap(y + way, NY), z, c)
        else:
            target = device(x, y, wrap(z + way, NZ), c)
        return pltpu.make_async_remote_copy(
            src_ref=ring_send.at[flow, step, sub],
            dst_ref=ring_recv.at[flow, step, sub],
            send_sem=ring_ssem.at[flow, step, sub],
            recv_sem=ring_rsem.at[flow, step, sub],
            device_id=target,
            device_id_type=MESH,
        )

    def partial(flow, step, sub):
        axis, way, g = FLOWS[flow]
        chunk = wrap(place(axis) - way * (1 + step), RING)
        if axis == "y":
            columns = g * HEAD + sub * HALF
            blocks = [acts_buf[chunk * NZL + i] for i in range(4)]
        else:
            columns = pl.multiple_of(g * HEAD + (chunk // NZL) * HALF, HALF)
            blocks = [acts_buf[(4 * sub + i) * NZL + lax.rem(chunk, NZL)] for i in range(4)]
        return jnp.dot(
            vgt_buf[pl.ds(columns, HALF), :],
            jnp.concatenate(blocks, axis=1),
            preferred_element_type=F32,
        )

    def ring_step(step, first):
        for sub in range(2):
            for flow in range(4):
                total = partial(flow, step, sub)
                if not first:
                    ring_copy(flow, step - 1, sub).wait_recv()
                    total += ring_recv[flow, step - 1, sub].astype(F32)
                ring_send[flow, step, sub] = total.astype(BF16)
                ring_copy(flow, step, sub).start()

    ring_step(0, True)

    load_values.wait()

    @pl.loop(0, KV_HEADS)
    def _(g):
        columns = pl.ds(pl.multiple_of(g * HEAD, HEAD), HEAD)
        values = v_ref[:, columns]
        total = jnp.zeros((BLOCK, HEAD), F32)
        for pair in range(GROUP // 2):
            first = g * GROUP * HEAD + pair * 2 * HEAD
            prob_grads = nt_dot(values, stacked(g_ref, first))
            probs = probs_buf[g * (GROUP // 2) + pair]
            row_dots = jnp.sum(
                probs.astype(BF16).astype(F32) * prob_grads, axis=0, keepdims=True
            )
            score_grads = (probs * (prob_grads - row_dots)).astype(BF16)
            total += jnp.dot(score_grads, stacked(q_ref, first), preferred_element_type=F32)
        key_ref[:, columns] = (total * factor).astype(BF16)

    @pl.loop(1, RING - 1)
    def _(step):
        ring_step(step, False)

    last = RING - 1
    for sub in range(2):
        for flow in range(4):
            total = partial(flow, last, sub)
            ring_copy(flow, last - 1, sub).wait_recv()
            total = (total + ring_recv[flow, last - 1, sub].astype(F32)).astype(BF16)
            for i in range(4):
                piece = total[:, i * BLOCK : (i + 1) * BLOCK]
                if FLOWS[flow][0] == "y":
                    zx_send[sub * NZL + i, flow] = piece
                else:
                    yx_send[4 * sub + i, flow - 2] = piece

    def zx_copy(to, slot, i):
        return pltpu.make_async_remote_copy(
            src_ref=zx_send.at[to], dst_ref=zx_recv.at[slot],
            send_sem=zx_ssem.at[i], recv_sem=zx_rsem.at[slot],
            device_id=device(x, y, to, c), device_id_type=MESH,
        )

    def yx_copy(to, slot, i):
        return pltpu.make_async_remote_copy(
            src_ref=yx_send.at[to], dst_ref=yx_recv.at[slot],
            send_sem=yx_ssem.at[i], recv_sem=yx_rsem.at[slot],
            device_id=device(x, to, z, c), device_id_type=MESH,
        )

    for i in range(1, RING):
        zx_copy(wrap(z + i, NZ), z, i).start()
        yx_copy(wrap(y + i, NY), y, i).start()
    zx_recv[z] = zx_send[z]
    yx_recv[y] = yx_send[y]
    for i in range(1, RING):
        zx_copy(wrap(z + i, NZ), wrap(z - i, NZ), i).wait_recv()
        yx_copy(wrap(y + i, NY), wrap(y - i, NY), i).wait_recv()
    zx_total = zx_recv[0].astype(F32)
    yx_total = yx_recv[0].astype(F32)
    for i in range(1, RING):
        zx_total += zx_recv[i].astype(F32)
        yx_total += yx_recv[i].astype(F32)
    x_send[0:2] = zx_total.astype(BF16)
    x_send[2:4] = yx_total.astype(BF16)

    def x_copy(to, slot, i):
        return pltpu.make_async_remote_copy(
            src_ref=x_send.at[to], dst_ref=x_recv.at[slot],
            send_sem=x_ssem.at[i], recv_sem=x_rsem.at[slot],
            device_id=device(to, y, z, c), device_id_type=MESH,
        )

    for i in range(1, NX):
        x_copy(wrap(x + i, NX), x, i).start()
    x_recv[x] = x_send[x]
    for i in range(1, NX):
        x_copy(wrap(x + i, NX), wrap(x - i, NX), i).wait_recv()
    final = x_recv[0].astype(F32)
    for i in range(1, NX):
        final += x_recv[i].astype(F32)
    final = final * (1.0 / math.sqrt(BLOCK * f_count * NX * CORES * (NZ // NZL)))

    def gather_copy(from_x, from_zh, to_x, to_zh, i, slot):
        rows = pl.ds(pl.multiple_of(from_x * HEAD + from_zh * HALF, HALF), HALF)
        return pltpu.make_async_remote_copy(
            src_ref=window.at[1 + c, rows], dst_ref=window.at[1 + c, rows],
            send_sem=gather_ssem.at[i], recv_sem=gather_rsem.at[slot],
            device_id=device(to_x, y, to_zh * NZL + zl, c), device_id_type=MESH,
        )

    own_rows = pl.ds(pl.multiple_of(x * HEAD + zh * HALF, HALF), HALF)
    window[1 + c, own_rows] = final.astype(BF16)
    moves = [(i, j) for j in (1, 0) for i in range(NX) if i or j]
    for n, (i, j) in enumerate(moves):
        to_x, to_zh = wrap(x + i, NX), wrap(zh + j, 2)
        gather_copy(x, zh, to_x, to_zh, n, zh * NX + x).start()
    for n, (i, j) in enumerate(moves):
        from_x, from_zh = wrap(x - i, NX), wrap(zh - j, 2)
        gather_copy(from_x, from_zh, x, zh, n, from_zh * NX + from_x).wait_recv()

    def spread_copy(block, slot, target):
        return pltpu.make_async_remote_copy(
            src_ref=window.at[1 + c], dst_ref=window.at[block],
            send_sem=spread_ssem.at[slot], recv_sem=spread_rsem.at[slot],
            device_id=target, device_id_type=MESH,
        )

    outer = 3 * (1 - c)

    def outer_copy(n, target):
        return pltpu.make_async_remote_copy(
            src_ref=window.at[1 + c], dst_ref=window.at[outer],
            send_sem=spread_ssem.at[1 + n], recv_sem=spread_rsem.at[1 + c],
            device_id=target, device_id_type=MESH,
        )

    outer_copy(0, (rep, far)).start()
    outer_copy(1, (rep + 1 - 2 * c, far)).start()
    spread_copy(1 + c, 0, sibling).start()

    pltpu.make_async_copy(window.at[2 - c], window.at[2 - c], spread_rsem.at[0]).wait()
    pltpu.make_async_copy(window.at[3], window.at[3], spread_rsem.at[1]).wait()
    pltpu.make_async_copy(window.at[0], window.at[0], spread_rsem.at[2]).wait()
    first_row = table_ref[0, 0] - (2 * BLOCK * fsdp - BLOCK)
    columns = jnp.concatenate([window[block] for block in range(4)], axis=1)
    for start in range(0, slot_ref.shape[0], HALF):
        row = start + lax.broadcasted_iota(jnp.int32, (HALF, 4 * BLOCK), 0)
        source = lax.broadcasted_iota(jnp.int32, (HALF, 4 * BLOCK), 1)
        chosen = (source == row + first_row) & (row < table_ref[0, 1])
        slot_ref[start : start + HALF, :] = nt_dot(
            jnp.where(chosen, 1.0, 0.0).astype(BF16), columns
        ).astype(BF16)

    pltpu.make_async_copy(far_half, far_half, acts_sems.at[0]).wait()
    vg_copy.wait_send()

    @pl.loop(0, RING - 1)
    def _(step):
        for flow in range(4):
            for sub in range(2):
                ring_copy(flow, step, sub).wait_send()

    for i in range(1, RING):
        zx_copy(wrap(z + i, NZ), z, i).wait_send()
        yx_copy(wrap(y + i, NY), y, i).wait_send()
    for i in range(1, NX):
        x_copy(wrap(x + i, NX), x, i).wait_send()
    for n, (i, j) in enumerate(moves):
        gather_copy(x, zh, wrap(x + i, NX), wrap(zh + j, 2), n, zh * NX + x).wait_send()
    outer_copy(0, (rep, far)).wait_send()
    outer_copy(1, (rep + 1 - 2 * c, far)).wait_send()
    spread_copy(1 + c, 0, sibling).wait_send()


def shards(activations, queries, keys, values, out_grad, positions, shard_table):
    tokens, width = keys.shape
    stride = activations.shape[1] // lax.axis_size("fsdp")
    slot_rows = stride + stride // 4
    vmem = pl.BlockSpec(memory_space=pltpu.VMEM)
    hbm = pl.BlockSpec(memory_space=pltpu.HBM)
    dma = pltpu.SemaphoreType.DMA
    ring = (4, RING - 1, 2)
    key_grad, slot_grad = pl.pallas_call(
        kernel,
        out_shape=(
            jax.ShapeDtypeStruct((tokens, width), BF16),
            jax.ShapeDtypeStruct((slot_rows, width), BF16),
        ),
        in_specs=[pl.BlockSpec(memory_space=pltpu.SMEM), vmem] + [hbm] * 5,
        out_specs=(vmem, vmem),
        scratch_shapes=[
            pltpu.VMEM(queries.shape, BF16),
            pltpu.VMEM(keys.shape, BF16),
            pltpu.VMEM(values.shape, BF16),
            pltpu.VMEM(out_grad.shape, BF16),
            pltpu.VMEM((NY * NZL, 2 * BLOCK, BLOCK), BF16),
            pltpu.VMEM((width, 2 * BLOCK), BF16),
            pltpu.VMEM((KV_HEADS * GROUP // 2, BLOCK, 2 * BLOCK), F32),
            pltpu.VMEM(ring + (HALF, 4 * BLOCK), BF16),
            pltpu.VMEM(ring + (HALF, 4 * BLOCK), BF16),
            pltpu.VMEM((NZ, 2, HALF, BLOCK), BF16),
            pltpu.VMEM((NZ, 2, HALF, BLOCK), BF16),
            pltpu.VMEM((NY, 2, HALF, BLOCK), BF16),
            pltpu.VMEM((NY, 2, HALF, BLOCK), BF16),
            pltpu.VMEM((NX, HALF, BLOCK), BF16),
            pltpu.VMEM((NX, HALF, BLOCK), BF16),
            pltpu.VMEM((4, width, BLOCK), BF16),
            dma((10,)), dma((1,)), dma((2,)), dma((2,)), dma(ring), dma(ring),
            dma((RING,)), dma((RING,)), dma((RING,)), dma((RING,)), dma((NX,)), dma((NX,)),
            dma((RING,)), dma((RING,)), dma((3,)), dma((3,)),
        ],
        compiler_params=pltpu.CompilerParams(
            collective_id=0, has_side_effects=True, vmem_limit_bytes=62 * 1024 * 1024
        ),
        cost_estimate=pl.CostEstimate(
            flops=2 * 10**9, bytes_accessed=6 * 2**20, transcendentals=2**19
        ),
    )(
        shard_table.reshape(1, 2), positions.reshape(1, tokens),
        queries, keys, values, out_grad, activations,
    )
    return (key_grad, slot_grad.reshape(1, 1, slot_rows, width))


def solution(mesh):
    return jax.shard_map(
        shards,
        mesh=mesh,
        in_specs=(
            P(("rep", "fsdp"), None),
            P(("rep", "fsdp"), None),
            P(("rep", "fsdp"), None),
            P(("rep", "fsdp"), None),
            P(("rep", "fsdp"), None),
            P(("rep", "fsdp")),
            P("rep", "fsdp", None),
        ),
        out_specs=(P(("rep", "fsdp"), None), P("rep", "fsdp", None, None)),
        check_vma=False,
    )
```

```python
import math

import jax
import jax.numpy as jnp
from jax import lax
from jax.experimental import pallas as pl
from jax.experimental.pallas import tpu as pltpu
from jax.sharding import PartitionSpec as P

HEAD = 128
GROUP = 8
KV_HEADS = 4
NX, NY, NZ, NZL, CORES = 4, 8, 8, 4, 2
RING = 8
BLOCK = 128
HALF = 64
BF16, F32 = jnp.bfloat16, jnp.float32
MESH = pl.DeviceIdType.MESH
AXES = ("y", "y", "z", "z")
HOPS = 4
FLOWS = tuple((g, 1 - 2 * (g % 2), HOPS) for g in range(KV_HEADS)) + tuple(
    (g, 2 * (g % 2) - 1, HOPS - 1) for g in range(KV_HEADS)
)


def device(x, y, z, c):
    zh, zl = z // NZL, lax.rem(z, NZL)
    return ((zh * NX + x) * CORES + c, y * NZL + zl)


def wrap(value, size):
    return lax.rem(value + 2 * size, size)


def nt_dot(a, b):
    return lax.dot_general(a, b, (((1,), (1,)), ((), ())), preferred_element_type=F32)


def kernel(
    table_ref, pos_ref, q_hbm, k_hbm, v_hbm, g_hbm, acts_ref,
    key_ref, slot_ref,
    q_ref, k_ref, v_ref, g_ref, acts_buf, vgt_buf, probs_buf, ring_send, ring_recv,
    zx_send, zx_recv, yx_send, yx_recv, x_send, x_recv, window,
    load_sems, local_sem, acts_sems, vg_sems, ring_ssem, ring_rsem,
    zx_ssem, zx_rsem, yx_ssem, yx_rsem, x_ssem, x_rsem,
    gather_ssem, gather_rsem, spread_ssem, spread_rsem,
):
    rep, fsdp = lax.axis_index("rep"), lax.axis_index("fsdp")
    c = lax.rem(rep, CORES)
    x = lax.rem(rep // CORES, NX)
    zh = rep // (CORES * NX)
    y, zl = fsdp // NZL, lax.rem(fsdp, NZL)
    z = zh * NZL + zl
    sibling = device(x, y, z, 1 - c)
    f_count = NY * NZL

    def beside(way, core):
        edge = jnp.where(zl == (NZL - 1 if way == 1 else 0), way, 0)
        return device(x, wrap(y + edge, NY), wrap(z + way, NZ), core)

    heads = KV_HEADS * HEAD
    span = GROUP * HEAD

    def load(n, source, target, first, size):
        part = pl.ds(first, size)
        return pltpu.make_async_copy(source.at[:, part], target.at[:, part], load_sems.at[n])

    load_keys = load(0, k_hbm, k_ref, 0, heads)
    load_values = load(1, v_hbm, v_ref, 0, heads)
    load_queries = [load(2 + g, q_hbm, q_ref, g * span, span) for g in range(KV_HEADS)]
    load_grads = [load(6 + g, g_hbm, g_ref, g * span, span) for g in range(KV_HEADS)]
    load_keys.start()
    for g in range(KV_HEADS):
        load_queries[g].start()
        load_grads[g].start()
    load_values.start()

    partners = [sibling]
    partners += [device(x, wrap(y + i, NY), z, c) for i in range(1, NY)]
    partners += [device(x, y, wrap(z + i, NZ), c) for i in range(1, NZ)]
    partners += [device(wrap(x + i, NX), y, z, c) for i in range(1, NX)]
    partners += [device(wrap(x + i, NX), y, wrap(z + NZL, NZ), c) for i in range(1, NX)]
    partners += [beside(way, core) for way in (1, -1) for core in (0, 1)]
    barrier = pltpu.get_barrier_semaphore()
    for partner in partners:
        pl.semaphore_signal(barrier, inc=1, device_id=partner, device_id_type=MESH)

    def local_acts(f):
        return pltpu.make_async_copy(
            acts_ref.at[:, pl.ds(pl.multiple_of(2 * BLOCK * f + BLOCK * c, BLOCK), BLOCK)],
            acts_buf.at[f, pl.ds(0, BLOCK)],
            local_sem.at[0],
        )

    def send_acts(f):
        return pltpu.make_async_remote_copy(
            src_ref=acts_ref.at[
                :, pl.ds(pl.multiple_of(2 * BLOCK * f + BLOCK * (1 - c), BLOCK), BLOCK)
            ],
            dst_ref=acts_buf.at[f, pl.ds(BLOCK, BLOCK)],
            send_sem=acts_sems.at[0],
            recv_sem=acts_sems.at[1],
            device_id=sibling,
            device_id_type=MESH,
        )

    @pl.loop(0, f_count)
    def _(f):
        local_acts(f).start()

    factor = 1.0 / math.sqrt(HEAD)
    key_index = lax.broadcasted_iota(jnp.int32, (BLOCK, BLOCK), 0)
    query_index = lax.broadcasted_iota(jnp.int32, (BLOCK, BLOCK), 1)
    allowed = (key_index <= query_index) & (key_index >= query_index - pos_ref[...])
    allowed = jnp.concatenate((allowed, allowed), axis=1)

    def stacked(ref, first):
        return jnp.concatenate(
            [ref[:, pl.ds(pl.multiple_of(first + i * HEAD, HEAD), HEAD)] for i in range(2)], axis=0
        )

    def values_of(g):
        keys = k_ref[:, pl.ds(pl.multiple_of(g * HEAD, HEAD), HEAD)]
        total = jnp.zeros((BLOCK, HEAD), F32)
        for pair in range(GROUP // 2):
            first = g * GROUP * HEAD + pair * 2 * HEAD
            scores = nt_dot(keys, stacked(q_ref, first)) * factor
            scores = jnp.where(allowed, scores, -1e30)
            raised = jnp.exp(scores - jnp.max(scores, axis=0, keepdims=True))
            probs = raised / jnp.sum(raised, axis=0, keepdims=True)
            probs_buf[g * (GROUP // 2) + pair] = probs
            total += jnp.dot(
                probs.astype(BF16), stacked(g_ref, first), preferred_element_type=F32
            )
        vgt_buf[pl.ds(pl.multiple_of(g * HEAD, HEAD), HEAD), pl.ds(0, BLOCK)] = total.T.astype(BF16)

    load_keys.wait()
    for g in range(2):
        load_queries[g].wait()
        load_grads[g].wait()

    @pl.loop(0, 2)
    def _(g):
        values_of(g)

    pl.semaphore_wait(barrier, len(partners))

    @pl.loop(0, f_count)
    def _(f):
        send_acts(f).start()

    for g in range(2, KV_HEADS):
        load_queries[g].wait()
        load_grads[g].wait()

    @pl.loop(2, KV_HEADS)
    def _(g):
        values_of(g)

    vg_copy = pltpu.make_async_remote_copy(
        src_ref=vgt_buf.at[:, pl.ds(0, BLOCK)],
        dst_ref=vgt_buf.at[:, pl.ds(BLOCK, BLOCK)],
        send_sem=vg_sems.at[0],
        recv_sem=vg_sems.at[1],
        device_id=sibling,
        device_id_type=MESH,
    )
    vg_copy.start()
    own_half = acts_buf.at[:, pl.ds(0, BLOCK)]
    far_half = acts_buf.at[:, pl.ds(BLOCK, BLOCK)]
    pltpu.make_async_copy(own_half, own_half, local_sem.at[0]).wait()
    pltpu.make_async_copy(far_half, far_half, acts_sems.at[1]).wait()
    vg_copy.wait_recv()

    def place(axis):
        return y if axis == "y" else z

    def ring_copy(flow, step, sub):
        g, way, _ = FLOWS[flow]
        if AXES[g] == "y":
            target = device(x, wrap(y + way, NY), z, c)
        else:
            target = device(x, y, wrap(z + way, NZ), c)
        return pltpu.make_async_remote_copy(
            src_ref=ring_send.at[flow, step, sub],
            dst_ref=ring_recv.at[flow, step, sub],
            send_sem=ring_ssem.at[flow, step, sub],
            recv_sem=ring_rsem.at[flow, step, sub],
            device_id=target,
            device_id_type=MESH,
        )

    def partial(g, distance, sub):
        chunk = wrap(place(AXES[g]) + distance, RING)
        if AXES[g] == "y":
            columns = g * HEAD + sub * HALF
            blocks = [acts_buf[chunk * NZL + i] for i in range(4)]
        else:
            columns = pl.multiple_of(g * HEAD + (chunk // NZL) * HALF, HALF)
            blocks = [acts_buf[(4 * sub + i) * NZL + lax.rem(chunk, NZL)] for i in range(4)]
        return jnp.dot(
            vgt_buf[pl.ds(columns, HALF), :],
            jnp.concatenate(blocks, axis=1),
            preferred_element_type=F32,
        )

    def ring_step(step, flows, first=False):
        for half in range(0, flows, KV_HEADS):
            for sub in range(2):
                for flow in range(half, half + KV_HEADS):
                    g, way, hops = FLOWS[flow]
                    total = partial(g, way * (hops - step), sub)
                    if not first:
                        ring_copy(flow, step - 1, sub).wait_recv()
                        total += ring_recv[flow, step - 1, sub].astype(F32)
                    ring_send[flow, step, sub] = total.astype(BF16)
                    ring_copy(flow, step, sub).start()

    ring_step(0, 2 * KV_HEADS, True)

    load_values.wait()

    @pl.loop(0, KV_HEADS)
    def _(g):
        columns = pl.ds(pl.multiple_of(g * HEAD, HEAD), HEAD)
        values = v_ref[:, columns]
        total = jnp.zeros((BLOCK, HEAD), F32)
        for pair in range(GROUP // 2):
            first = g * GROUP * HEAD + pair * 2 * HEAD
            prob_grads = nt_dot(values, stacked(g_ref, first))
            probs = probs_buf[g * (GROUP // 2) + pair]
            row_dots = jnp.sum(
                probs.astype(BF16).astype(F32) * prob_grads, axis=0, keepdims=True
            )
            score_grads = (probs * (prob_grads - row_dots)).astype(BF16)
            total += jnp.dot(score_grads, stacked(q_ref, first), preferred_element_type=F32)
        key_ref[:, columns] = (total * factor).astype(BF16)

    @pl.loop(1, HOPS - 1)
    def _(step):
        ring_step(step, 2 * KV_HEADS)

    ring_step(HOPS - 1, KV_HEADS)
    for sub in range(2):
        for g in range(KV_HEADS):
            total = partial(g, 0, sub)
            for flow in (g + KV_HEADS, g):
                hops = FLOWS[flow][2]
                ring_copy(flow, hops - 1, sub).wait_recv()
                total += ring_recv[flow, hops - 1, sub].astype(F32)
            total = total.astype(BF16)
            for i in range(4):
                piece = total[:, i * BLOCK : (i + 1) * BLOCK]
                if AXES[g] == "y":
                    zx_send[sub * NZL + i, g] = piece
                else:
                    yx_send[4 * sub + i, g - 2] = piece

    def zx_copy(to, slot, i):
        return pltpu.make_async_remote_copy(
            src_ref=zx_send.at[to], dst_ref=zx_recv.at[slot],
            send_sem=zx_ssem.at[i], recv_sem=zx_rsem.at[slot],
            device_id=device(x, y, to, c), device_id_type=MESH,
        )

    def yx_copy(to, slot, i):
        return pltpu.make_async_remote_copy(
            src_ref=yx_send.at[to], dst_ref=yx_recv.at[slot],
            send_sem=yx_ssem.at[i], recv_sem=yx_rsem.at[slot],
            device_id=device(x, to, z, c), device_id_type=MESH,
        )

    for i in range(1, RING):
        zx_copy(wrap(z + i, NZ), z, i).start()
        yx_copy(wrap(y + i, NY), y, i).start()
    zx_recv[z] = zx_send[z]
    yx_recv[y] = yx_send[y]
    for i in range(1, RING):
        zx_copy(wrap(z + i, NZ), wrap(z - i, NZ), i).wait_recv()
        yx_copy(wrap(y + i, NY), wrap(y - i, NY), i).wait_recv()
    zx_total = zx_recv[0].astype(F32)
    yx_total = yx_recv[0].astype(F32)
    for i in range(1, RING):
        zx_total += zx_recv[i].astype(F32)
        yx_total += yx_recv[i].astype(F32)
    x_send[0:2] = zx_total.astype(BF16)
    x_send[2:4] = yx_total.astype(BF16)

    def x_copy(to, slot, i):
        return pltpu.make_async_remote_copy(
            src_ref=x_send.at[to], dst_ref=x_recv.at[slot],
            send_sem=x_ssem.at[i], recv_sem=x_rsem.at[slot],
            device_id=device(to, y, z, c), device_id_type=MESH,
        )

    for i in range(1, NX):
        x_copy(wrap(x + i, NX), x, i).start()
    x_recv[x] = x_send[x]
    for i in range(1, NX):
        x_copy(wrap(x + i, NX), wrap(x - i, NX), i).wait_recv()
    final = x_recv[0].astype(F32)
    for i in range(1, NX):
        final += x_recv[i].astype(F32)
    final = final * (1.0 / math.sqrt(BLOCK * f_count * NX * CORES * (NZ // NZL)))

    def gather_copy(from_x, from_zh, to_x, to_zh, i, slot):
        rows = pl.ds(pl.multiple_of(from_x * HEAD + from_zh * HALF, HALF), HALF)
        return pltpu.make_async_remote_copy(
            src_ref=window.at[1 + c, rows], dst_ref=window.at[1 + c, rows],
            send_sem=gather_ssem.at[i], recv_sem=gather_rsem.at[slot],
            device_id=device(to_x, y, to_zh * NZL + zl, c), device_id_type=MESH,
        )

    own_rows = pl.ds(pl.multiple_of(x * HEAD + zh * HALF, HALF), HALF)
    window[1 + c, own_rows] = final.astype(BF16)
    moves = [(i, j) for j in (1, 0) for i in range(NX) if i or j]
    for n, (i, j) in enumerate(moves):
        to_x, to_zh = wrap(x + i, NX), wrap(zh + j, 2)
        gather_copy(x, zh, to_x, to_zh, n, zh * NX + x).start()
    for n, (i, j) in enumerate(moves):
        from_x, from_zh = wrap(x - i, NX), wrap(zh - j, 2)
        gather_copy(from_x, from_zh, x, zh, n, from_zh * NX + from_x).wait_recv()

    def spread_copy(block, slot, target):
        return pltpu.make_async_remote_copy(
            src_ref=window.at[1 + c], dst_ref=window.at[block],
            send_sem=spread_ssem.at[slot], recv_sem=spread_rsem.at[slot],
            device_id=target, device_id_type=MESH,
        )

    outer = 3 * (1 - c)

    def outer_copy(n, target):
        return pltpu.make_async_remote_copy(
            src_ref=window.at[1 + c], dst_ref=window.at[outer],
            send_sem=spread_ssem.at[1 + n], recv_sem=spread_rsem.at[1 + c],
            device_id=target, device_id_type=MESH,
        )

    before = [beside(-1, core) for core in (0, 1)]
    after = [beside(1, core) for core in (0, 1)]
    targets = [tuple(jnp.where(c == 0, a, b) for a, b in zip(before[n], after[n])) for n in (0, 1)]
    outer_copy(0, targets[0]).start()
    outer_copy(1, targets[1]).start()
    spread_copy(1 + c, 0, sibling).start()

    pltpu.make_async_copy(far_half, far_half, acts_sems.at[0]).wait()
    vg_copy.wait_send()
    for flow in range(2 * KV_HEADS):
        for step in range(FLOWS[flow][2]):
            for sub in range(2):
                ring_copy(flow, step, sub).wait_send()
    for i in range(1, RING):
        zx_copy(wrap(z + i, NZ), z, i).wait_send()
        yx_copy(wrap(y + i, NY), y, i).wait_send()
    for i in range(1, NX):
        x_copy(wrap(x + i, NX), x, i).wait_send()
    for n, (i, j) in enumerate(moves):
        gather_copy(x, zh, wrap(x + i, NX), wrap(zh + j, 2), n, zh * NX + x).wait_send()

    pltpu.make_async_copy(window.at[2 - c], window.at[2 - c], spread_rsem.at[0]).wait()
    pltpu.make_async_copy(window.at[3], window.at[3], spread_rsem.at[1]).wait()
    pltpu.make_async_copy(window.at[0], window.at[0], spread_rsem.at[2]).wait()
    first_row = table_ref[0, 0] - (2 * BLOCK * fsdp - BLOCK)
    columns = jnp.concatenate([window[block] for block in range(4)], axis=1)
    for start in range(0, slot_ref.shape[0], HALF):
        row = start + lax.broadcasted_iota(jnp.int32, (HALF, 4 * BLOCK), 0)
        source = lax.broadcasted_iota(jnp.int32, (HALF, 4 * BLOCK), 1)
        chosen = (source == row + first_row) & (row < table_ref[0, 1])
        slot_ref[start : start + HALF, :] = nt_dot(
            jnp.where(chosen, 1.0, 0.0).astype(BF16), columns
        ).astype(BF16)

    outer_copy(0, targets[0]).wait_send()
    outer_copy(1, targets[1]).wait_send()
    spread_copy(1 + c, 0, sibling).wait_send()


def shards(activations, queries, keys, values, out_grad, positions, shard_table):
    tokens, width = keys.shape
    stride = activations.shape[1] // lax.axis_size("fsdp")
    slot_rows = stride + stride // 4
    vmem = pl.BlockSpec(memory_space=pltpu.VMEM)
    hbm = pl.BlockSpec(memory_space=pltpu.HBM)
    dma = pltpu.SemaphoreType.DMA
    ring = (2 * KV_HEADS, HOPS, 2)
    key_grad, slot_grad = pl.pallas_call(
        kernel,
        out_shape=(
            pltpu.VMEM((tokens, width), BF16),
            pltpu.VMEM((slot_rows, width), BF16),
        ),
        in_specs=[pl.BlockSpec(memory_space=pltpu.SMEM), vmem] + [hbm] * 5,
        out_specs=(vmem, vmem),
        scratch_shapes=[
            pltpu.VMEM(queries.shape, BF16),
            pltpu.VMEM(keys.shape, BF16),
            pltpu.VMEM(values.shape, BF16),
            pltpu.VMEM(out_grad.shape, BF16),
            pltpu.VMEM((NY * NZL, 2 * BLOCK, BLOCK), BF16),
            pltpu.VMEM((width, 2 * BLOCK), BF16),
            pltpu.VMEM((KV_HEADS * GROUP // 2, BLOCK, 2 * BLOCK), F32),
            pltpu.VMEM(ring + (HALF, 4 * BLOCK), BF16),
            pltpu.VMEM(ring + (HALF, 4 * BLOCK), BF16),
            pltpu.VMEM((NZ, 2, HALF, BLOCK), BF16),
            pltpu.VMEM((NZ, 2, HALF, BLOCK), BF16),
            pltpu.VMEM((NY, 2, HALF, BLOCK), BF16),
            pltpu.VMEM((NY, 2, HALF, BLOCK), BF16),
            pltpu.VMEM((NX, HALF, BLOCK), BF16),
            pltpu.VMEM((NX, HALF, BLOCK), BF16),
            pltpu.VMEM((4, width, BLOCK), BF16),
            dma((10,)), dma((1,)), dma((2,)), dma((2,)), dma(ring), dma(ring),
            dma((RING,)), dma((RING,)), dma((RING,)), dma((RING,)), dma((NX,)), dma((NX,)),
            dma((RING,)), dma((RING,)), dma((3,)), dma((3,)),
        ],
        compiler_params=pltpu.CompilerParams(
            collective_id=0, has_side_effects=True, vmem_limit_bytes=62 * 1024 * 1024
        ),
        cost_estimate=pl.CostEstimate(
            flops=2 * 10**9, bytes_accessed=6 * 2**20, transcendentals=2**19
        ),
    )(
        shard_table.reshape(1, 2), positions.reshape(1, tokens),
        queries, keys, values, out_grad, activations,
    )
    return (key_grad, slot_grad.reshape(1, 1, slot_rows, width))


def solution(mesh):
    return jax.shard_map(
        shards,
        mesh=mesh,
        in_specs=(
            P(("rep", "fsdp"), None),
            P(("rep", "fsdp"), None),
            P(("rep", "fsdp"), None),
            P(("rep", "fsdp"), None),
            P(("rep", "fsdp"), None),
            P(("rep", "fsdp")),
            P("rep", "fsdp", None),
        ),
        out_specs=(P(("rep", "fsdp"), None), P("rep", "fsdp", None, None)),
        check_vma=False,
    )
```

```python
import math

import jax
import jax.numpy as jnp
from jax import lax
from jax.experimental import pallas as pl
from jax.experimental.pallas import tpu as pltpu
from jax.sharding import PartitionSpec as P

HEAD = 128
GROUP = 8
KV_HEADS = 4
NX, NY, NZ, NZL, CORES = 4, 8, 8, 4, 2
RING = 8
BLOCK = 128
HALF = 64
BF16, F32 = jnp.bfloat16, jnp.float32
MESH = pl.DeviceIdType.MESH
AXES = ("y", "y", "z", "z")
HOPS = 4
FLOWS = tuple((g, 1 - 2 * (g % 2), HOPS) for g in range(KV_HEADS)) + tuple(
    (g, 2 * (g % 2) - 1, HOPS - 1) for g in range(KV_HEADS)
)


def device(x, y, z, c):
    zh, zl = z // NZL, lax.rem(z, NZL)
    return ((zh * NX + x) * CORES + c, y * NZL + zl)


def wrap(value, size):
    return lax.rem(value + 2 * size, size)


def nt_dot(a, b):
    return lax.dot_general(a, b, (((1,), (1,)), ((), ())), preferred_element_type=F32)


def kernel(
    table_ref, pos_ref, q_hbm, k_hbm, v_hbm, g_hbm, acts_ref,
    key_ref, slot_ref,
    q_ref, k_ref, v_ref, g_ref, acts_buf, vgt_buf, probs_buf, ring_send, ring_recv,
    zx_send, zx_recv, yx_send, yx_recv, x_send, x_recv, window, chosen_buf, slot_buf,
    load_sems, local_sem, acts_sems, vg_sems, ring_ssem, ring_rsem,
    zx_ssem, zx_rsem, yx_ssem, yx_rsem, x_ssem, x_rsem,
    gather_ssem, gather_rsem, spread_ssem, spread_rsem,
):
    rep, fsdp = lax.axis_index("rep"), lax.axis_index("fsdp")
    c = lax.rem(rep, CORES)
    x = lax.rem(rep // CORES, NX)
    zh = rep // (CORES * NX)
    y, zl = fsdp // NZL, lax.rem(fsdp, NZL)
    z = zh * NZL + zl
    sibling = device(x, y, z, 1 - c)
    f_count = NY * NZL

    def beside(way, core):
        edge = jnp.where(zl == (NZL - 1 if way == 1 else 0), way, 0)
        return device(x, wrap(y + edge, NY), wrap(z + way, NZ), core)

    heads = KV_HEADS * HEAD
    span = GROUP * HEAD

    def load(n, source, target, first, size):
        part = pl.ds(first, size)
        return pltpu.make_async_copy(source.at[:, part], target.at[:, part], load_sems.at[n])

    load_keys = load(0, k_hbm, k_ref, 0, heads)
    load_values = load(1, v_hbm, v_ref, 0, heads)
    load_queries = [load(2 + g, q_hbm, q_ref, g * span, span) for g in range(KV_HEADS)]
    load_grads = [load(6 + g, g_hbm, g_ref, g * span, span) for g in range(KV_HEADS)]
    load_keys.start()
    for g in range(KV_HEADS):
        load_queries[g].start()
        load_grads[g].start()
    load_values.start()

    partners = [sibling]
    partners += [device(x, wrap(y + i, NY), z, c) for i in (1, -1)]
    partners += [device(x, y, wrap(z + i, NZ), c) for i in (1, -1)]
    partners += [device(wrap(x + i, NX), y, z, c) for i in range(1, NX)]
    barrier = pltpu.get_barrier_semaphore()
    for partner in partners:
        pl.semaphore_signal(barrier, inc=1, device_id=partner, device_id_type=MESH)

    def local_acts(f):
        return pltpu.make_async_copy(
            acts_ref.at[:, pl.ds(pl.multiple_of(2 * BLOCK * f + BLOCK * c, BLOCK), BLOCK)],
            acts_buf.at[f, pl.ds(0, BLOCK)],
            local_sem.at[0],
        )

    def send_acts(f):
        return pltpu.make_async_remote_copy(
            src_ref=acts_ref.at[
                :, pl.ds(pl.multiple_of(2 * BLOCK * f + BLOCK * (1 - c), BLOCK), BLOCK)
            ],
            dst_ref=acts_buf.at[f, pl.ds(BLOCK, BLOCK)],
            send_sem=acts_sems.at[0],
            recv_sem=acts_sems.at[1],
            device_id=sibling,
            device_id_type=MESH,
        )

    @pl.loop(0, f_count)
    def _(f):
        local_acts(f).start()

    factor = 1.0 / math.sqrt(HEAD)
    key_index = lax.broadcasted_iota(jnp.int32, (BLOCK, BLOCK), 0)
    query_index = lax.broadcasted_iota(jnp.int32, (BLOCK, BLOCK), 1)
    allowed = (key_index <= query_index) & (key_index >= query_index - pos_ref[...])
    allowed = jnp.concatenate((allowed, allowed), axis=1)

    def stacked(ref, first):
        return jnp.concatenate(
            [ref[:, pl.ds(pl.multiple_of(first + i * HEAD, HEAD), HEAD)] for i in range(2)], axis=0
        )

    def values_of(g):
        keys = k_ref[:, pl.ds(pl.multiple_of(g * HEAD, HEAD), HEAD)]
        total = jnp.zeros((BLOCK, HEAD), F32)
        for pair in range(GROUP // 2):
            first = g * GROUP * HEAD + pair * 2 * HEAD
            scores = nt_dot(keys, stacked(q_ref, first)) * factor
            scores = jnp.where(allowed, scores, -1e30)
            raised = jnp.exp(scores - jnp.max(scores, axis=0, keepdims=True))
            probs = raised / jnp.sum(raised, axis=0, keepdims=True)
            probs_buf[g * (GROUP // 2) + pair] = probs
            total += jnp.dot(
                probs.astype(BF16), stacked(g_ref, first), preferred_element_type=F32
            )
        vgt_buf[pl.ds(pl.multiple_of(g * HEAD, HEAD), HEAD), pl.ds(0, BLOCK)] = total.T.astype(BF16)

    load_keys.wait()
    for g in range(2):
        load_queries[g].wait()
        load_grads[g].wait()

    @pl.loop(0, 2)
    def _(g):
        values_of(g)

    for g in range(2, KV_HEADS):
        load_queries[g].wait()
        load_grads[g].wait()

    @pl.loop(2, KV_HEADS)
    def _(g):
        values_of(g)

    pl.semaphore_wait(barrier, len(partners))

    @pl.loop(0, f_count)
    def _(f):
        send_acts(f).start()

    vg_copy = pltpu.make_async_remote_copy(
        src_ref=vgt_buf.at[:, pl.ds(0, BLOCK)],
        dst_ref=vgt_buf.at[:, pl.ds(BLOCK, BLOCK)],
        send_sem=vg_sems.at[0],
        recv_sem=vg_sems.at[1],
        device_id=sibling,
        device_id_type=MESH,
    )
    vg_copy.start()
    own_half = acts_buf.at[:, pl.ds(0, BLOCK)]
    far_half = acts_buf.at[:, pl.ds(BLOCK, BLOCK)]
    pltpu.make_async_copy(own_half, own_half, local_sem.at[0]).wait()
    pltpu.make_async_copy(far_half, far_half, acts_sems.at[1]).wait()
    vg_copy.wait_recv()

    def place(axis):
        return y if axis == "y" else z

    def ring_copy(flow, step, sub):
        g, way, _ = FLOWS[flow]
        if AXES[g] == "y":
            target = device(x, wrap(y + way, NY), z, c)
        else:
            target = device(x, y, wrap(z + way, NZ), c)
        return pltpu.make_async_remote_copy(
            src_ref=ring_send.at[flow, step, sub],
            dst_ref=ring_recv.at[flow, step, sub],
            send_sem=ring_ssem.at[flow, step, sub],
            recv_sem=ring_rsem.at[flow, step, sub],
            device_id=target,
            device_id_type=MESH,
        )

    def partial(g, distance, sub):
        chunk = wrap(place(AXES[g]) + distance, RING)
        if AXES[g] == "y":
            columns = g * HEAD + sub * HALF
            blocks = [acts_buf[chunk * NZL + i] for i in range(4)]
        else:
            columns = pl.multiple_of(g * HEAD + (chunk // NZL) * HALF, HALF)
            blocks = [acts_buf[(4 * sub + i) * NZL + lax.rem(chunk, NZL)] for i in range(4)]
        return jnp.dot(
            vgt_buf[pl.ds(columns, HALF), :],
            jnp.concatenate(blocks, axis=1),
            preferred_element_type=F32,
        )

    def ring_step(step, flows, first=False):
        for sub in range(2):
            for half in range(0, flows, KV_HEADS):
                for flow in range(half, half + KV_HEADS):
                    g, way, hops = FLOWS[flow]
                    total = partial(g, way * (hops - step), sub)
                    if not first:
                        ring_copy(flow, step - 1, sub).wait_recv()
                        total += ring_recv[flow, step - 1, sub].astype(F32)
                    ring_send[flow, step, sub] = total.astype(BF16)
                    ring_copy(flow, step, sub).start()

    ring_step(0, 2 * KV_HEADS, True)

    @pl.loop(1, HOPS - 1)
    def _(step):
        ring_step(step, 2 * KV_HEADS)

    def zx_copy(to, slot):
        return pltpu.make_async_remote_copy(
            src_ref=zx_send.at[to], dst_ref=zx_recv.at[slot],
            send_sem=zx_ssem.at[to], recv_sem=zx_rsem.at[slot],
            device_id=device(x, y, to, c), device_id_type=MESH,
        )

    def yx_copy(to, slot):
        return pltpu.make_async_remote_copy(
            src_ref=yx_send.at[to], dst_ref=yx_recv.at[slot],
            send_sem=yx_ssem.at[to], recv_sem=yx_rsem.at[slot],
            device_id=device(x, to, z, c), device_id_type=MESH,
        )

    ring_step(HOPS - 1, KV_HEADS)
    for sub in range(2):
        for g in range(KV_HEADS):
            total = partial(g, 0, sub)
            for flow in (g + KV_HEADS, g):
                hops = FLOWS[flow][2]
                ring_copy(flow, hops - 1, sub).wait_recv()
                total += ring_recv[flow, hops - 1, sub].astype(F32)
            total = total.astype(BF16)
            for i in range(4):
                piece = total[:, i * BLOCK : (i + 1) * BLOCK]
                if AXES[g] == "y":
                    zx_send[sub * NZL + i, g] = piece
                else:
                    yx_send[4 * sub + i, g - 2] = piece
        for i in range(4):
            to_z, to_y = 4 * sub + lax.rem(z + i, 4), 4 * sub + lax.rem(y + i, 4)

            @pl.when(to_z != z)
            def _():
                zx_copy(to_z, z).start()

            @pl.when(to_y != y)
            def _():
                yx_copy(to_y, y).start()

    first_row = table_ref[0, 0] - (2 * BLOCK * fsdp - BLOCK)
    for start in range(0, slot_ref.shape[0], HALF):
        row = start + lax.broadcasted_iota(jnp.int32, (HALF, 4 * BLOCK), 0)
        source = lax.broadcasted_iota(jnp.int32, (HALF, 4 * BLOCK), 1)
        chosen = (source == row + first_row) & (row < table_ref[0, 1])
        chosen_buf[pl.ds(start, HALF), :] = jnp.where(chosen, 1.0, 0.0).astype(BF16)

    zx_recv[z] = zx_send[z]
    yx_recv[y] = yx_send[y]

    load_values.wait()

    @pl.loop(0, KV_HEADS)
    def _(g):
        columns = pl.ds(pl.multiple_of(g * HEAD, HEAD), HEAD)
        values = v_ref[:, columns]
        total = jnp.zeros((BLOCK, HEAD), F32)
        for pair in range(GROUP // 2):
            first = g * GROUP * HEAD + pair * 2 * HEAD
            prob_grads = nt_dot(values, stacked(g_ref, first))
            probs = probs_buf[g * (GROUP // 2) + pair]
            row_dots = jnp.sum(
                probs.astype(BF16).astype(F32) * prob_grads, axis=0, keepdims=True
            )
            score_grads = (probs * (prob_grads - row_dots)).astype(BF16)
            total += jnp.dot(score_grads, stacked(q_ref, first), preferred_element_type=F32)
        key_ref[:, columns] = (total * factor).astype(BF16)

    for i in range(1, RING):
        zx_copy(wrap(z + i, NZ), wrap(z - i, NZ)).wait_recv()
        yx_copy(wrap(y + i, NY), wrap(y - i, NY)).wait_recv()
    zx_total = zx_recv[0].astype(F32)
    yx_total = yx_recv[0].astype(F32)
    for i in range(1, RING):
        zx_total += zx_recv[i].astype(F32)
        yx_total += yx_recv[i].astype(F32)
    x_send[0:2] = zx_total.astype(BF16)
    x_send[2:4] = yx_total.astype(BF16)

    def x_copy(to, slot, i):
        return pltpu.make_async_remote_copy(
            src_ref=x_send.at[to], dst_ref=x_recv.at[slot],
            send_sem=x_ssem.at[i], recv_sem=x_rsem.at[slot],
            device_id=device(to, y, z, c), device_id_type=MESH,
        )

    for i in range(1, NX):
        x_copy(wrap(x + i, NX), x, i).start()
    x_recv[x] = x_send[x]
    for i in range(1, NX):
        x_copy(wrap(x + i, NX), wrap(x - i, NX), i).wait_recv()
    final = x_recv[0].astype(F32)
    for i in range(1, NX):
        final += x_recv[i].astype(F32)
    final = final * (1.0 / math.sqrt(BLOCK * f_count * NX * CORES * (NZ // NZL)))

    def gather_copy(from_x, from_zh, to_x, to_zh, i, slot):
        rows = pl.ds(pl.multiple_of((from_zh * NX + from_x) * HALF, HALF), HALF)
        return pltpu.make_async_remote_copy(
            src_ref=window.at[1 + c, rows], dst_ref=window.at[1 + c, rows],
            send_sem=gather_ssem.at[i], recv_sem=gather_rsem.at[slot],
            device_id=device(to_x, y, to_zh * NZL + zl, c), device_id_type=MESH,
        )

    own_rows = pl.ds(pl.multiple_of((zh * NX + x) * HALF, HALF), HALF)
    window[1 + c, own_rows] = final.astype(BF16)
    moves = [(i, j) for j in (1, 0) for i in range(NX) if i or j]
    for n, (i, j) in enumerate(moves):
        to_x, to_zh = wrap(x + i, NX), wrap(zh + j, 2)
        gather_copy(x, zh, to_x, to_zh, n, zh * NX + x).start()
    before = [beside(-1, core) for core in (0, 1)]
    after = [beside(1, core) for core in (0, 1)]
    targets = [tuple(jnp.where(c == 0, a, b) for a, b in zip(before[n], after[n])) for n in (0, 1)]
    targets.append(sibling)
    outer = 3 * (1 - c)

    def spread_copy(half, n):
        rows = pl.ds(pl.multiple_of(half * NX * HALF, HALF), NX * HALF)
        block, slot = (1 + c, 2) if n == 2 else (outer, c)
        return pltpu.make_async_remote_copy(
            src_ref=window.at[1 + c, rows], dst_ref=window.at[block, rows],
            send_sem=spread_ssem.at[half, n], recv_sem=spread_rsem.at[half, slot],
            device_id=targets[n], device_id_type=MESH,
        )

    for far_half_too in (0, 1):
        for n, (i, j) in enumerate(moves):
            if j == far_half_too:
                from_x, from_zh = wrap(x - i, NX), wrap(zh - j, 2)
                gather_copy(from_x, from_zh, x, zh, n, from_zh * NX + from_x).wait_recv()
        for n in range(3):
            spread_copy(wrap(zh + far_half_too, 2), n).start()

    pltpu.make_async_copy(far_half, far_half, acts_sems.at[0]).wait()
    vg_copy.wait_send()
    for flow in range(2 * KV_HEADS):
        for step in range(FLOWS[flow][2]):
            for sub in range(2):
                ring_copy(flow, step, sub).wait_send()
    for i in range(1, RING):
        zx_copy(wrap(z + i, NZ), z).wait_send()
        yx_copy(wrap(y + i, NY), y).wait_send()
    for i in range(1, NX):
        x_copy(wrap(x + i, NX), x, i).wait_send()
    for n, (i, j) in enumerate(moves):
        gather_copy(x, zh, wrap(x + i, NX), wrap(zh + j, 2), n, zh * NX + x).wait_send()

    def ordered(block):
        parts = [
            window[block, (h * NX + g) * HALF : (h * NX + g + 1) * HALF, :]
            for g in range(NX)
            for h in range(2)
        ]
        return jnp.concatenate(parts, axis=0)

    def picked(start, blocks):
        columns = jnp.concatenate([ordered(block) for block in blocks], axis=1)
        part = jnp.concatenate(
            [chosen_buf[pl.ds(start, HALF), pl.ds(block * BLOCK, BLOCK)] for block in blocks],
            axis=1,
        )
        return nt_dot(part, columns)

    def arrived(block, slot):
        for half in range(2):
            part = window.at[block, pl.ds(half * NX * HALF, NX * HALF)]
            pltpu.make_async_copy(part, part, spread_rsem.at[half, slot]).wait()

    starts = range(0, slot_ref.shape[0], HALF)
    arrived(2 - c, 2)
    for start in starts:
        slot_buf[pl.ds(start, HALF), :] = picked(start, (1, 2))
    arrived(3, 0)
    arrived(0, 1)
    for start in starts:
        rows = pl.ds(start, HALF)
        slot_ref[rows, :] = (slot_buf[rows, :] + picked(start, (0, 3))).astype(BF16)

    for half in range(2):
        for n in range(3):
            spread_copy(half, n).wait_send()


def shards(activations, queries, keys, values, out_grad, positions, shard_table):
    tokens, width = keys.shape
    stride = activations.shape[1] // lax.axis_size("fsdp")
    slot_rows = stride + stride // 4
    vmem = pl.BlockSpec(memory_space=pltpu.VMEM)
    hbm = pl.BlockSpec(memory_space=pltpu.HBM)
    dma = pltpu.SemaphoreType.DMA
    ring = (2 * KV_HEADS, HOPS, 2)
    key_grad, slot_grad = pl.pallas_call(
        kernel,
        out_shape=(
            pltpu.VMEM((tokens, width), BF16),
            pltpu.VMEM((slot_rows, width), BF16),
        ),
        in_specs=[pl.BlockSpec(memory_space=pltpu.SMEM), vmem] + [hbm] * 5,
        out_specs=(vmem, vmem),
        scratch_shapes=[
            pltpu.VMEM(queries.shape, BF16),
            pltpu.VMEM(keys.shape, BF16),
            pltpu.VMEM(values.shape, BF16),
            pltpu.VMEM(out_grad.shape, BF16),
            pltpu.VMEM((NY * NZL, 2 * BLOCK, BLOCK), BF16),
            pltpu.VMEM((width, 2 * BLOCK), BF16),
            pltpu.VMEM((KV_HEADS * GROUP // 2, BLOCK, 2 * BLOCK), F32),
            pltpu.VMEM(ring + (HALF, 4 * BLOCK), BF16),
            pltpu.VMEM(ring + (HALF, 4 * BLOCK), BF16),
            pltpu.VMEM((NZ, 2, HALF, BLOCK), BF16),
            pltpu.VMEM((NZ, 2, HALF, BLOCK), BF16),
            pltpu.VMEM((NY, 2, HALF, BLOCK), BF16),
            pltpu.VMEM((NY, 2, HALF, BLOCK), BF16),
            pltpu.VMEM((NX, HALF, BLOCK), BF16),
            pltpu.VMEM((NX, HALF, BLOCK), BF16),
            pltpu.VMEM((4, width, BLOCK), BF16),
            pltpu.VMEM((slot_rows, 4 * BLOCK), BF16),
            pltpu.VMEM((slot_rows, width), F32),
            dma((10,)), dma((1,)), dma((2,)), dma((2,)), dma(ring), dma(ring),
            dma((RING,)), dma((RING,)), dma((RING,)), dma((RING,)), dma((NX,)), dma((NX,)),
            dma((RING,)), dma((RING,)), dma((2, 3)), dma((2, 3)),
        ],
        compiler_params=pltpu.CompilerParams(
            collective_id=0, has_side_effects=True, vmem_limit_bytes=62 * 1024 * 1024
        ),
        cost_estimate=pl.CostEstimate(
            flops=2 * 10**9, bytes_accessed=6 * 2**20, transcendentals=2**19
        ),
    )(
        shard_table.reshape(1, 2), positions.reshape(1, tokens),
        queries, keys, values, out_grad, activations,
    )
    return (key_grad, slot_grad.reshape(1, 1, slot_rows, width))


def solution(mesh):
    return jax.shard_map(
        shards,
        mesh=mesh,
        in_specs=(
            P(("rep", "fsdp"), None),
            P(("rep", "fsdp"), None),
            P(("rep", "fsdp"), None),
            P(("rep", "fsdp"), None),
            P(("rep", "fsdp"), None),
            P(("rep", "fsdp")),
            P("rep", "fsdp", None),
        ),
        out_specs=(P(("rep", "fsdp"), None), P("rep", "fsdp", None, None)),
        check_vma=False,
    )
```

```python
import math

import jax
import jax.numpy as jnp
from jax import lax
from jax.experimental import pallas as pl
from jax.experimental.pallas import tpu as pltpu
from jax.sharding import PartitionSpec as P

HEAD = 128
GROUP = 8
KV_HEADS = 4
NX, NY, NZ, NZL, CORES = 4, 8, 8, 4, 2
RING = 8
BLOCK = 128
HALF = 64
PICK = 160
BF16, F32 = jnp.bfloat16, jnp.float32
MESH = pl.DeviceIdType.MESH
AXES = ("y", "y", "z", "z")
HOPS = 4
FLOWS = tuple((g, 1 - 2 * (g % 2), HOPS) for g in range(KV_HEADS)) + tuple(
    (g, 2 * (g % 2) - 1, HOPS - 1) for g in range(KV_HEADS)
)


def device(x, y, z, c):
    zh, zl = z // NZL, lax.rem(z, NZL)
    return ((zh * NX + x) * CORES + c, y * NZL + zl)


def wrap(value, size):
    return lax.rem(value + 2 * size, size)


def nt_dot(a, b):
    return lax.dot_general(a, b, (((1,), (1,)), ((), ())), preferred_element_type=F32)


def kernel(
    table_ref, pos_ref, q_hbm, k_hbm, v_hbm, g_hbm, acts_ref,
    key_ref, slot_ref,
    q_ref, k_ref, v_ref, g_ref, acts_buf, vgt_buf, probs_buf, ring_send, ring_recv,
    zx_send, zx_recv, yx_send, yx_recv, x_send, x_recv, window, chosen_buf, slot_buf,
    load_sems, local_sem, acts_sems, vg_sems, ring_ssem, ring_rsem,
    zx_ssem, zx_rsem, yx_ssem, yx_rsem, x_ssem, x_rsem,
    gather_ssem, gather_rsem, spread_ssem, spread_rsem,
):
    rep, fsdp = lax.axis_index("rep"), lax.axis_index("fsdp")
    c = lax.rem(rep, CORES)
    x = lax.rem(rep // CORES, NX)
    zh = rep // (CORES * NX)
    y, zl = fsdp // NZL, lax.rem(fsdp, NZL)
    z = zh * NZL + zl
    sibling = device(x, y, z, 1 - c)
    f_count = NY * NZL

    def beside(way, core):
        edge = jnp.where(zl == (NZL - 1 if way == 1 else 0), way, 0)
        return device(x, wrap(y + edge, NY), wrap(z + way, NZ), core)

    heads = KV_HEADS * HEAD
    span = GROUP * HEAD

    def load(n, source, target, first, size):
        part = pl.ds(first, size)
        return pltpu.make_async_copy(source.at[:, part], target.at[:, part], load_sems.at[n])

    load_keys = load(0, k_hbm, k_ref, 0, heads)
    load_values = load(1, v_hbm, v_ref, 0, heads)
    load_queries = [load(2 + g, q_hbm, q_ref, g * span, span) for g in range(KV_HEADS)]
    load_grads = [load(6 + g, g_hbm, g_ref, g * span, span) for g in range(KV_HEADS)]
    load_keys.start()
    for g in range(KV_HEADS):
        load_queries[g].start()
        load_grads[g].start()
    load_values.start()

    partners = [sibling]
    partners += [device(x, wrap(y + i, NY), z, c) for i in (1, -1)]
    partners += [device(x, y, wrap(z + i, NZ), c) for i in (1, -1)]
    partners += [device(wrap(x + i, NX), y, z, c) for i in range(1, NX)]
    barrier = pltpu.get_barrier_semaphore()
    for partner in partners:
        pl.semaphore_signal(barrier, inc=1, device_id=partner, device_id_type=MESH)

    def local_acts(f):
        return pltpu.make_async_copy(
            acts_ref.at[:, pl.ds(pl.multiple_of(2 * BLOCK * f + BLOCK * c, BLOCK), BLOCK)],
            acts_buf.at[f, pl.ds(0, BLOCK)],
            local_sem.at[0],
        )

    def send_acts(f):
        return pltpu.make_async_remote_copy(
            src_ref=acts_ref.at[
                :, pl.ds(pl.multiple_of(2 * BLOCK * f + BLOCK * (1 - c), BLOCK), BLOCK)
            ],
            dst_ref=acts_buf.at[f, pl.ds(BLOCK, BLOCK)],
            send_sem=acts_sems.at[0],
            recv_sem=acts_sems.at[1],
            device_id=sibling,
            device_id_type=MESH,
        )

    @pl.loop(0, f_count)
    def _(f):
        local_acts(f).start()

    factor = 1.0 / math.sqrt(HEAD)
    key_index = lax.broadcasted_iota(jnp.int32, (BLOCK, BLOCK), 0)
    query_index = lax.broadcasted_iota(jnp.int32, (BLOCK, BLOCK), 1)
    allowed = (key_index <= query_index) & (key_index >= query_index - pos_ref[...])
    allowed = jnp.concatenate((allowed, allowed), axis=1)

    def stacked(ref, first):
        return jnp.concatenate(
            [ref[:, pl.ds(pl.multiple_of(first + i * HEAD, HEAD), HEAD)] for i in range(2)], axis=0
        )

    def values_of(g):
        keys = k_ref[:, pl.ds(pl.multiple_of(g * HEAD, HEAD), HEAD)]
        total = jnp.zeros((BLOCK, HEAD), F32)
        for pair in range(GROUP // 2):
            first = g * GROUP * HEAD + pair * 2 * HEAD
            scores = nt_dot(keys, stacked(q_ref, first)) * factor
            scores = jnp.where(allowed, scores, -1e30)
            raised = jnp.exp(scores - jnp.max(scores, axis=0, keepdims=True))
            probs = raised / jnp.sum(raised, axis=0, keepdims=True)
            probs_buf[g * (GROUP // 2) + pair] = probs
            total += jnp.dot(
                probs.astype(BF16), stacked(g_ref, first), preferred_element_type=F32
            )
        vgt_buf[pl.ds(pl.multiple_of(g * HEAD, HEAD), HEAD), pl.ds(0, BLOCK)] = total.T.astype(BF16)

    load_keys.wait()
    for g in range(2):
        load_queries[g].wait()
        load_grads[g].wait()

    @pl.loop(0, 2)
    def _(g):
        values_of(g)

    for g in range(2, KV_HEADS):
        load_queries[g].wait()
        load_grads[g].wait()

    @pl.loop(2, KV_HEADS)
    def _(g):
        values_of(g)

    pl.semaphore_wait(barrier, len(partners))

    vg_copy = pltpu.make_async_remote_copy(
        src_ref=vgt_buf.at[:, pl.ds(0, BLOCK)],
        dst_ref=vgt_buf.at[:, pl.ds(BLOCK, BLOCK)],
        send_sem=vg_sems.at[0],
        recv_sem=vg_sems.at[1],
        device_id=sibling,
        device_id_type=MESH,
    )
    vg_copy.start()

    @pl.loop(0, f_count)
    def _(f):
        send_acts(f).start()

    own_half = acts_buf.at[:, pl.ds(0, BLOCK)]
    far_half = acts_buf.at[:, pl.ds(BLOCK, BLOCK)]
    pltpu.make_async_copy(own_half, own_half, local_sem.at[0]).wait()
    pltpu.make_async_copy(far_half, far_half, acts_sems.at[1]).wait()
    vg_copy.wait_recv()

    def place(axis):
        return y if axis == "y" else z

    def ring_copy(flow, step, sub):
        g, way, _ = FLOWS[flow]
        if AXES[g] == "y":
            target = device(x, wrap(y + way, NY), z, c)
        else:
            target = device(x, y, wrap(z + way, NZ), c)
        return pltpu.make_async_remote_copy(
            src_ref=ring_send.at[flow, step, sub],
            dst_ref=ring_recv.at[flow, step, sub],
            send_sem=ring_ssem.at[flow, step, sub],
            recv_sem=ring_rsem.at[flow, step, sub],
            device_id=target,
            device_id_type=MESH,
        )

    def partial(g, distance, sub):
        chunk = wrap(place(AXES[g]) + distance, RING)
        if AXES[g] == "y":
            columns = g * HEAD + sub * HALF
            blocks = [acts_buf[chunk * NZL + i] for i in range(4)]
        else:
            columns = pl.multiple_of(g * HEAD + (chunk // NZL) * HALF, HALF)
            blocks = [acts_buf[(4 * sub + i) * NZL + lax.rem(chunk, NZL)] for i in range(4)]
        return jnp.dot(
            vgt_buf[pl.ds(columns, HALF), :],
            jnp.concatenate(blocks, axis=1),
            preferred_element_type=F32,
        )

    def ring_step(step, flows, first=False):
        for sub in range(2):
            for half in range(0, flows, KV_HEADS):
                for flow in range(half, half + KV_HEADS):
                    g, way, hops = FLOWS[flow]
                    total = partial(g, way * (hops - step), sub)
                    if not first:
                        ring_copy(flow, step - 1, sub).wait_recv()
                        total += ring_recv[flow, step - 1, sub].astype(F32)
                    ring_send[flow, step, sub] = total.astype(BF16)
                    ring_copy(flow, step, sub).start()

    ring_step(0, 2 * KV_HEADS, True)

    @pl.loop(1, HOPS - 1)
    def _(step):
        ring_step(step, 2 * KV_HEADS)

    def zx_copy(to, slot):
        return pltpu.make_async_remote_copy(
            src_ref=zx_send.at[to], dst_ref=zx_recv.at[slot],
            send_sem=zx_ssem.at[to], recv_sem=zx_rsem.at[slot],
            device_id=device(x, y, to, c), device_id_type=MESH,
        )

    def yx_copy(to, slot):
        return pltpu.make_async_remote_copy(
            src_ref=yx_send.at[to], dst_ref=yx_recv.at[slot],
            send_sem=yx_ssem.at[to], recv_sem=yx_rsem.at[slot],
            device_id=device(x, to, z, c), device_id_type=MESH,
        )

    ring_step(HOPS - 1, KV_HEADS)
    for sub in range(2):
        for g in range(KV_HEADS):
            total = partial(g, 0, sub)
            for flow in (g + KV_HEADS, g):
                hops = FLOWS[flow][2]
                ring_copy(flow, hops - 1, sub).wait_recv()
                total += ring_recv[flow, hops - 1, sub].astype(F32)
            total = total.astype(BF16)
            for i in range(4):
                piece = total[:, i * BLOCK : (i + 1) * BLOCK]
                if AXES[g] == "y":
                    zx_send[sub * NZL + i, g] = piece
                else:
                    yx_send[4 * sub + i, g - 2] = piece
        for i in range(4):
            to_z, to_y = 4 * sub + lax.rem(z + i, 4), 4 * sub + lax.rem(y + i, 4)

            @pl.when(to_z != z)
            def _():
                zx_copy(to_z, z).start()

            @pl.when(to_y != y)
            def _():
                yx_copy(to_y, y).start()

    first_row = table_ref[0, 0] - (2 * BLOCK * fsdp - BLOCK)
    for start in range(0, slot_ref.shape[0], HALF):
        row = start + lax.broadcasted_iota(jnp.int32, (HALF, 4 * BLOCK), 0)
        source = lax.broadcasted_iota(jnp.int32, (HALF, 4 * BLOCK), 1)
        chosen = (source == row + first_row) & (row < table_ref[0, 1])
        chosen_buf[pl.ds(start, HALF), :] = jnp.where(chosen, 1.0, 0.0).astype(BF16)

    zx_recv[z] = zx_send[z]
    yx_recv[y] = yx_send[y]

    load_values.wait()

    @pl.loop(0, KV_HEADS)
    def _(g):
        columns = pl.ds(pl.multiple_of(g * HEAD, HEAD), HEAD)
        values = v_ref[:, columns]
        total = jnp.zeros((BLOCK, HEAD), F32)
        for pair in range(GROUP // 2):
            first = g * GROUP * HEAD + pair * 2 * HEAD
            prob_grads = nt_dot(values, stacked(g_ref, first))
            probs = probs_buf[g * (GROUP // 2) + pair]
            row_dots = jnp.sum(
                probs.astype(BF16).astype(F32) * prob_grads, axis=0, keepdims=True
            )
            score_grads = (probs * (prob_grads - row_dots)).astype(BF16)
            total += jnp.dot(score_grads, stacked(q_ref, first), preferred_element_type=F32)
        key_ref[:, columns] = (total * factor).astype(BF16)

    def x_copy(to, slot):
        return pltpu.make_async_remote_copy(
            src_ref=x_send.at[to], dst_ref=x_recv.at[slot],
            send_sem=x_ssem.at[to], recv_sem=x_rsem.at[slot],
            device_id=device(to, y, z, c), device_id_type=MESH,
        )

    def pass_on(total, first):
        x_send[first : first + 2] = total.astype(BF16)
        for to in (first, first + 1):

            @pl.when(to != x)
            def _():
                x_copy(to, x).start()

    for i in range(1, RING):
        yx_copy(wrap(y + i, NY), wrap(y - i, NY)).wait_recv()
    pass_on(sum(yx_recv[i].astype(F32) for i in range(RING)), 2)
    for i in range(1, RING):
        zx_copy(wrap(z + i, NZ), wrap(z - i, NZ)).wait_recv()
    pass_on(sum(zx_recv[i].astype(F32) for i in range(RING)), 0)
    x_recv[x] = x_send[x]
    for i in range(1, NX):
        x_copy(wrap(x + i, NX), wrap(x - i, NX)).wait_recv()
    final = x_recv[0].astype(F32)
    for i in range(1, NX):
        final += x_recv[i].astype(F32)
    final = final * (1.0 / math.sqrt(BLOCK * f_count * NX * CORES * (NZ // NZL)))

    def gather_copy(from_x, from_zh, to_x, to_zh, i, slot):
        rows = pl.ds(pl.multiple_of((from_zh * NX + from_x) * HALF, HALF), HALF)
        return pltpu.make_async_remote_copy(
            src_ref=window.at[1 + c, rows], dst_ref=window.at[1 + c, rows],
            send_sem=gather_ssem.at[i], recv_sem=gather_rsem.at[slot],
            device_id=device(to_x, y, to_zh * NZL + zl, c), device_id_type=MESH,
        )

    own_rows = pl.ds(pl.multiple_of((zh * NX + x) * HALF, HALF), HALF)
    window[1 + c, own_rows] = final.astype(BF16)
    moves = [(i, j) for j in (1, 0) for i in (2, 1, 3, 0) if i or j]
    for n, (i, j) in enumerate(moves):
        to_x, to_zh = wrap(x + i, NX), wrap(zh + j, 2)
        gather_copy(x, zh, to_x, to_zh, n, zh * NX + x).start()
    before = [beside(-1, core) for core in (0, 1)]
    after = [beside(1, core) for core in (0, 1)]
    targets = [tuple(jnp.where(c == 0, a, b) for a, b in zip(before[n], after[n])) for n in (0, 1)]
    targets.append(sibling)
    outer = 3 * (1 - c)

    def spread_copy(half, n):
        rows = pl.ds(pl.multiple_of(half * NX * HALF, HALF), NX * HALF)
        block, slot = (1 + c, 2) if n == 2 else (outer, c)
        return pltpu.make_async_remote_copy(
            src_ref=window.at[1 + c, rows], dst_ref=window.at[block, rows],
            send_sem=spread_ssem.at[half, n], recv_sem=spread_rsem.at[half, slot],
            device_id=targets[n], device_id_type=MESH,
        )

    for far_half_too in (0, 1):
        for n, (i, j) in enumerate(moves):
            if j == far_half_too:
                from_x, from_zh = wrap(x - i, NX), wrap(zh - j, 2)
                gather_copy(from_x, from_zh, x, zh, n, from_zh * NX + from_x).wait_recv()
        for n in range(3):
            spread_copy(wrap(zh + far_half_too, 2), n).start()

    pltpu.make_async_copy(far_half, far_half, acts_sems.at[0]).wait()
    vg_copy.wait_send()
    for flow in range(2 * KV_HEADS):
        for step in range(FLOWS[flow][2]):
            for sub in range(2):
                ring_copy(flow, step, sub).wait_send()
    for i in range(1, RING):
        zx_copy(wrap(z + i, NZ), z).wait_send()
        yx_copy(wrap(y + i, NY), y).wait_send()
    for i in range(1, NX):
        x_copy(wrap(x + i, NX), x).wait_send()
    for n, (i, j) in enumerate(moves):
        gather_copy(x, zh, wrap(x + i, NX), wrap(zh + j, 2), n, zh * NX + x).wait_send()

    def ordered(block):
        parts = [
            window[block, (h * NX + g) * HALF : (h * NX + g + 1) * HALF, :]
            for g in range(NX)
            for h in range(2)
        ]
        return jnp.concatenate(parts, axis=0)

    def picked(start, blocks):
        columns = jnp.concatenate([ordered(block) for block in blocks], axis=1)
        part = jnp.concatenate(
            [chosen_buf[pl.ds(start, PICK), pl.ds(block * BLOCK, BLOCK)] for block in blocks],
            axis=1,
        )
        return nt_dot(part, columns)

    def arrived(block, slot):
        for half in range(2):
            part = window.at[block, pl.ds(half * NX * HALF, NX * HALF)]
            pltpu.make_async_copy(part, part, spread_rsem.at[half, slot]).wait()

    starts = range(0, slot_ref.shape[0], PICK)
    arrived(2 - c, 2)
    for start in starts:
        slot_buf[pl.ds(start, PICK), :] = picked(start, (1, 2))
    arrived(3, 0)
    arrived(0, 1)
    for start in starts:
        rows = pl.ds(start, PICK)
        slot_ref[rows, :] = (slot_buf[rows, :] + picked(start, (0, 3))).astype(BF16)

    for half in range(2):
        for n in range(3):
            spread_copy(half, n).wait_send()


def shards(activations, queries, keys, values, out_grad, positions, shard_table):
    tokens, width = keys.shape
    stride = activations.shape[1] // lax.axis_size("fsdp")
    slot_rows = stride + stride // 4
    vmem = pl.BlockSpec(memory_space=pltpu.VMEM)
    hbm = pl.BlockSpec(memory_space=pltpu.HBM)
    dma = pltpu.SemaphoreType.DMA
    ring = (2 * KV_HEADS, HOPS, 2)
    key_grad, slot_grad = pl.pallas_call(
        kernel,
        out_shape=(
            pltpu.VMEM((tokens, width), BF16),
            pltpu.VMEM((slot_rows, width), BF16),
        ),
        in_specs=[pl.BlockSpec(memory_space=pltpu.SMEM), vmem] + [hbm] * 5,
        out_specs=(vmem, vmem),
        scratch_shapes=[
            pltpu.VMEM(queries.shape, BF16),
            pltpu.VMEM(keys.shape, BF16),
            pltpu.VMEM(values.shape, BF16),
            pltpu.VMEM(out_grad.shape, BF16),
            pltpu.VMEM((NY * NZL, 2 * BLOCK, BLOCK), BF16),
            pltpu.VMEM((width, 2 * BLOCK), BF16),
            pltpu.VMEM((KV_HEADS * GROUP // 2, BLOCK, 2 * BLOCK), F32),
            pltpu.VMEM(ring + (HALF, 4 * BLOCK), BF16),
            pltpu.VMEM(ring + (HALF, 4 * BLOCK), BF16),
            pltpu.VMEM((NZ, 2, HALF, BLOCK), BF16),
            pltpu.VMEM((NZ, 2, HALF, BLOCK), BF16),
            pltpu.VMEM((NY, 2, HALF, BLOCK), BF16),
            pltpu.VMEM((NY, 2, HALF, BLOCK), BF16),
            pltpu.VMEM((NX, HALF, BLOCK), BF16),
            pltpu.VMEM((NX, HALF, BLOCK), BF16),
            pltpu.VMEM((4, width, BLOCK), BF16),
            pltpu.VMEM((slot_rows, 4 * BLOCK), BF16),
            pltpu.VMEM((slot_rows, width), F32),
            dma((10,)), dma((1,)), dma((2,)), dma((2,)), dma(ring), dma(ring),
            dma((RING,)), dma((RING,)), dma((RING,)), dma((RING,)), dma((NX,)), dma((NX,)),
            dma((RING,)), dma((RING,)), dma((2, 3)), dma((2, 3)),
        ],
        compiler_params=pltpu.CompilerParams(
            collective_id=0, has_side_effects=True, vmem_limit_bytes=62 * 1024 * 1024
        ),
        cost_estimate=pl.CostEstimate(
            flops=2 * 10**9, bytes_accessed=6 * 2**20, transcendentals=2**19
        ),
    )(
        shard_table.reshape(1, 2), positions.reshape(1, tokens),
        queries, keys, values, out_grad, activations,
    )
    return (key_grad, slot_grad.reshape(1, 1, slot_rows, width))


def solution(mesh):
    return jax.shard_map(
        shards,
        mesh=mesh,
        in_specs=(
            P(("rep", "fsdp"), None),
            P(("rep", "fsdp"), None),
            P(("rep", "fsdp"), None),
            P(("rep", "fsdp"), None),
            P(("rep", "fsdp"), None),
            P(("rep", "fsdp")),
            P("rep", "fsdp", None),
        ),
        out_specs=(P(("rep", "fsdp"), None), P("rep", "fsdp", None, None)),
        check_vma=False,
    )
```

```python
import math

import jax
import jax.numpy as jnp
from jax import lax
from jax.experimental import pallas as pl
from jax.experimental.pallas import tpu as pltpu
from jax.sharding import PartitionSpec as P

HEAD = 128
GROUP = 8
KV_HEADS = 4
NX, NY, NZ, NZL, CORES = 4, 8, 8, 4, 2
RING = 8
BLOCK = 128
HALF = 64
PICK = 160
BF16, F32 = jnp.bfloat16, jnp.float32
MESH = pl.DeviceIdType.MESH
AXES = ("y", "y", "z", "z")
HOPS = 4
FLOWS = tuple((g, 1 - 2 * (g % 2), HOPS) for g in range(KV_HEADS)) + tuple(
    (g, 2 * (g % 2) - 1, HOPS - 1) for g in range(KV_HEADS)
)


def device(x, y, z, c):
    zh, zl = z // NZL, lax.rem(z, NZL)
    return ((zh * NX + x) * CORES + c, y * NZL + zl)


def wrap(value, size):
    return lax.rem(value + 2 * size, size)


def nt_dot(a, b):
    return lax.dot_general(a, b, (((1,), (1,)), ((), ())), preferred_element_type=F32)


def kernel(
    table_ref, pos_ref, q_hbm, k_hbm, v_hbm, g_hbm, acts_ref,
    key_ref, slot_ref,
    q_ref, k_ref, v_ref, g_ref, acts_buf, vgt_buf, probs_buf, ring_send, ring_recv,
    zx_send, zx_recv, yx_send, yx_recv, x_send, x_recv, window, chosen_buf, slot_buf,
    load_sems, local_sem, acts_sems, vg_sems, ring_ssem, ring_rsem,
    zx_ssem, zx_rsem, yx_ssem, yx_rsem, x_ssem, x_rsem,
    gather_ssem, gather_rsem, spread_ssem, spread_rsem,
):
    rep, fsdp = lax.axis_index("rep"), lax.axis_index("fsdp")
    c = lax.rem(rep, CORES)
    x = lax.rem(rep // CORES, NX)
    zh = rep // (CORES * NX)
    y, zl = fsdp // NZL, lax.rem(fsdp, NZL)
    z = zh * NZL + zl
    sibling = device(x, y, z, 1 - c)
    f_count = NY * NZL

    def beside(way, core):
        edge = jnp.where(zl == (NZL - 1 if way == 1 else 0), way, 0)
        return device(x, wrap(y + edge, NY), wrap(z + way, NZ), core)

    heads = KV_HEADS * HEAD
    span = GROUP * HEAD

    def load(n, source, target, first, size):
        part = pl.ds(first, size)
        return pltpu.make_async_copy(source.at[:, part], target.at[:, part], load_sems.at[n])

    load_keys = load(0, k_hbm, k_ref, 0, heads)
    load_values = load(1, v_hbm, v_ref, 0, heads)
    load_queries = [load(2 + g, q_hbm, q_ref, g * span, span) for g in range(KV_HEADS)]
    load_grads = [load(6 + g, g_hbm, g_ref, g * span, span) for g in range(KV_HEADS)]
    load_keys.start()
    for g in range(KV_HEADS):
        load_queries[g].start()
        load_grads[g].start()
    load_values.start()

    partners = [sibling]
    partners += [device(x, wrap(y + i, NY), z, c) for i in (1, -1)]
    partners += [device(x, y, wrap(z + i, NZ), c) for i in (1, -1)]
    partners += [device(wrap(x + i, NX), y, z, c) for i in range(1, NX)]
    barrier = pltpu.get_barrier_semaphore()
    for partner in partners:
        pl.semaphore_signal(barrier, inc=1, device_id=partner, device_id_type=MESH)

    def local_acts(f):
        return pltpu.make_async_copy(
            acts_ref.at[:, pl.ds(pl.multiple_of(2 * BLOCK * f + BLOCK * c, BLOCK), BLOCK)],
            acts_buf.at[f, pl.ds(0, BLOCK)],
            local_sem.at[0],
        )

    def send_acts(f):
        return pltpu.make_async_remote_copy(
            src_ref=acts_ref.at[
                :, pl.ds(pl.multiple_of(2 * BLOCK * f + BLOCK * (1 - c), BLOCK), BLOCK)
            ],
            dst_ref=acts_buf.at[f, pl.ds(BLOCK, BLOCK)],
            send_sem=acts_sems.at[0],
            recv_sem=acts_sems.at[1],
            device_id=sibling,
            device_id_type=MESH,
        )

    @pl.loop(0, f_count)
    def _(f):
        local_acts(f).start()

    factor = 1.0 / math.sqrt(HEAD)
    key_index = lax.broadcasted_iota(jnp.int32, (BLOCK, BLOCK), 0)
    query_index = lax.broadcasted_iota(jnp.int32, (BLOCK, BLOCK), 1)
    allowed = (key_index <= query_index) & (key_index >= query_index - pos_ref[...])
    allowed = jnp.concatenate((allowed, allowed), axis=1)

    def stacked(ref, first):
        return jnp.concatenate(
            [ref[:, pl.ds(pl.multiple_of(first + i * HEAD, HEAD), HEAD)] for i in range(2)], axis=0
        )

    def values_of(g):
        keys = k_ref[:, pl.ds(pl.multiple_of(g * HEAD, HEAD), HEAD)]
        total = jnp.zeros((BLOCK, HEAD), F32)
        for pair in range(GROUP // 2):
            first = g * GROUP * HEAD + pair * 2 * HEAD
            scores = nt_dot(keys, stacked(q_ref, first)) * factor
            scores = jnp.where(allowed, scores, -1e30)
            raised = jnp.exp(scores - jnp.max(scores, axis=0, keepdims=True))
            probs = raised / jnp.sum(raised, axis=0, keepdims=True)
            probs_buf[g * (GROUP // 2) + pair] = probs
            total += jnp.dot(
                probs.astype(BF16), stacked(g_ref, first), preferred_element_type=F32
            )
        vgt_buf[pl.ds(pl.multiple_of(g * HEAD, HEAD), HEAD), pl.ds(0, BLOCK)] = total.T.astype(BF16)

    load_keys.wait()
    for g in range(2):
        load_queries[g].wait()
        load_grads[g].wait()

    @pl.loop(0, 2)
    def _(g):
        values_of(g)

    pl.semaphore_wait(barrier, len(partners))

    @pl.loop(0, f_count)
    def _(f):
        send_acts(f).start()

    for g in range(2, KV_HEADS):
        load_queries[g].wait()
        load_grads[g].wait()

    @pl.loop(2, KV_HEADS)
    def _(g):
        values_of(g)


    vg_copy = pltpu.make_async_remote_copy(
        src_ref=vgt_buf.at[:, pl.ds(0, BLOCK)],
        dst_ref=vgt_buf.at[:, pl.ds(BLOCK, BLOCK)],
        send_sem=vg_sems.at[0],
        recv_sem=vg_sems.at[1],
        device_id=sibling,
        device_id_type=MESH,
    )
    vg_copy.start()

    own_half = acts_buf.at[:, pl.ds(0, BLOCK)]
    far_half = acts_buf.at[:, pl.ds(BLOCK, BLOCK)]
    pltpu.make_async_copy(own_half, own_half, local_sem.at[0]).wait()
    pltpu.make_async_copy(far_half, far_half, acts_sems.at[1]).wait()
    vg_copy.wait_recv()

    def place(axis):
        return y if axis == "y" else z

    def ring_copy(flow, step, sub):
        g, way, _ = FLOWS[flow]
        if AXES[g] == "y":
            target = device(x, wrap(y + way, NY), z, c)
        else:
            target = device(x, y, wrap(z + way, NZ), c)
        return pltpu.make_async_remote_copy(
            src_ref=ring_send.at[flow, step, sub],
            dst_ref=ring_recv.at[flow, step, sub],
            send_sem=ring_ssem.at[flow, step, sub],
            recv_sem=ring_rsem.at[flow, step, sub],
            device_id=target,
            device_id_type=MESH,
        )

    def partial(g, distance, sub):
        chunk = wrap(place(AXES[g]) + distance, RING)
        if AXES[g] == "y":
            columns = g * HEAD + sub * HALF
            blocks = [acts_buf[chunk * NZL + i] for i in range(4)]
        else:
            columns = pl.multiple_of(g * HEAD + (chunk // NZL) * HALF, HALF)
            blocks = [acts_buf[(4 * sub + i) * NZL + lax.rem(chunk, NZL)] for i in range(4)]
        return jnp.dot(
            vgt_buf[pl.ds(columns, HALF), :],
            jnp.concatenate(blocks, axis=1),
            preferred_element_type=F32,
        )

    def ring_step(step, flows, first=False):
        for sub in range(2):
            for half in range(0, flows, KV_HEADS):
                for flow in range(half, half + KV_HEADS):
                    g, way, hops = FLOWS[flow]
                    total = partial(g, way * (hops - step), sub)
                    if not first:
                        ring_copy(flow, step - 1, sub).wait_recv()
                        total += ring_recv[flow, step - 1, sub].astype(F32)
                    ring_send[flow, step, sub] = total.astype(BF16)
                    ring_copy(flow, step, sub).start()

    ring_step(0, 2 * KV_HEADS, True)

    @pl.loop(1, HOPS - 1)
    def _(step):
        ring_step(step, 2 * KV_HEADS)

    def zx_copy(to, slot):
        return pltpu.make_async_remote_copy(
            src_ref=zx_send.at[to], dst_ref=zx_recv.at[slot],
            send_sem=zx_ssem.at[to], recv_sem=zx_rsem.at[slot],
            device_id=device(x, y, to, c), device_id_type=MESH,
        )

    def yx_copy(to, slot):
        return pltpu.make_async_remote_copy(
            src_ref=yx_send.at[to], dst_ref=yx_recv.at[slot],
            send_sem=yx_ssem.at[to], recv_sem=yx_rsem.at[slot],
            device_id=device(x, to, z, c), device_id_type=MESH,
        )

    ring_step(HOPS - 1, KV_HEADS)
    for sub in range(2):
        for g in range(KV_HEADS):
            total = partial(g, 0, sub)
            for flow in (g + KV_HEADS, g):
                hops = FLOWS[flow][2]
                ring_copy(flow, hops - 1, sub).wait_recv()
                total += ring_recv[flow, hops - 1, sub].astype(F32)
            total = total.astype(BF16)
            for i in range(4):
                piece = total[:, i * BLOCK : (i + 1) * BLOCK]
                if AXES[g] == "y":
                    zx_send[sub * NZL + i, g] = piece
                else:
                    yx_send[4 * sub + i, g - 2] = piece
        for i in range(4):
            to_z, to_y = 4 * sub + lax.rem(z + i, 4), 4 * sub + lax.rem(y + i, 4)

            @pl.when(to_z != z)
            def _():
                zx_copy(to_z, z).start()

            @pl.when(to_y != y)
            def _():
                yx_copy(to_y, y).start()

    first_row = table_ref[0, 0] - (2 * BLOCK * fsdp - BLOCK)
    for start in range(0, slot_ref.shape[0], HALF):
        row = start + lax.broadcasted_iota(jnp.int32, (HALF, 4 * BLOCK), 0)
        source = lax.broadcasted_iota(jnp.int32, (HALF, 4 * BLOCK), 1)
        chosen = (source == row + first_row) & (row < table_ref[0, 1])
        chosen_buf[pl.ds(start, HALF), :] = jnp.where(chosen, 1.0, 0.0).astype(BF16)

    zx_recv[z] = zx_send[z]
    yx_recv[y] = yx_send[y]

    load_values.wait()

    @pl.loop(0, KV_HEADS)
    def _(g):
        columns = pl.ds(pl.multiple_of(g * HEAD, HEAD), HEAD)
        values = v_ref[:, columns]
        total = jnp.zeros((BLOCK, HEAD), F32)
        for pair in range(GROUP // 2):
            first = g * GROUP * HEAD + pair * 2 * HEAD
            prob_grads = nt_dot(values, stacked(g_ref, first))
            probs = probs_buf[g * (GROUP // 2) + pair]
            row_dots = jnp.sum(
                probs.astype(BF16).astype(F32) * prob_grads, axis=0, keepdims=True
            )
            score_grads = (probs * (prob_grads - row_dots)).astype(BF16)
            total += jnp.dot(score_grads, stacked(q_ref, first), preferred_element_type=F32)
        key_ref[:, columns] = (total * factor).astype(BF16)

    def x_copy(to, slot):
        return pltpu.make_async_remote_copy(
            src_ref=x_send.at[to], dst_ref=x_recv.at[slot],
            send_sem=x_ssem.at[to], recv_sem=x_rsem.at[slot],
            device_id=device(to, y, z, c), device_id_type=MESH,
        )

    def pass_on(total, first):
        x_send[first : first + 2] = total.astype(BF16)
        for to in (first, first + 1):

            @pl.when(to != x)
            def _():
                x_copy(to, x).start()

    for i in range(1, RING):
        yx_copy(wrap(y + i, NY), wrap(y - i, NY)).wait_recv()
    pass_on(sum(yx_recv[i].astype(F32) for i in range(RING)), 2)
    for i in range(1, RING):
        zx_copy(wrap(z + i, NZ), wrap(z - i, NZ)).wait_recv()
    pass_on(sum(zx_recv[i].astype(F32) for i in range(RING)), 0)
    x_recv[x] = x_send[x]
    for i in range(1, NX):
        x_copy(wrap(x + i, NX), wrap(x - i, NX)).wait_recv()
    final = x_recv[0].astype(F32)
    for i in range(1, NX):
        final += x_recv[i].astype(F32)
    final = final * (1.0 / math.sqrt(BLOCK * f_count * NX * CORES * (NZ // NZL)))

    def gather_copy(from_x, from_zh, to_x, to_zh, i, slot):
        rows = pl.ds(pl.multiple_of((from_zh * NX + from_x) * HALF, HALF), HALF)
        return pltpu.make_async_remote_copy(
            src_ref=window.at[1 + c, rows], dst_ref=window.at[1 + c, rows],
            send_sem=gather_ssem.at[i], recv_sem=gather_rsem.at[slot],
            device_id=device(to_x, y, to_zh * NZL + zl, c), device_id_type=MESH,
        )

    own_rows = pl.ds(pl.multiple_of((zh * NX + x) * HALF, HALF), HALF)
    window[1 + c, own_rows] = final.astype(BF16)
    moves = [(i, j) for j in (1, 0) for i in (2, 1, 3, 0) if i or j]
    for n, (i, j) in enumerate(moves):
        to_x, to_zh = wrap(x + i, NX), wrap(zh + j, 2)
        gather_copy(x, zh, to_x, to_zh, n, zh * NX + x).start()
    before = [beside(-1, core) for core in (0, 1)]
    after = [beside(1, core) for core in (0, 1)]
    targets = [tuple(jnp.where(c == 0, a, b) for a, b in zip(before[n], after[n])) for n in (0, 1)]
    targets.append(sibling)
    outer = 3 * (1 - c)

    def spread_copy(half, n):
        rows = pl.ds(pl.multiple_of(half * NX * HALF, HALF), NX * HALF)
        block, slot = (1 + c, 2) if n == 2 else (outer, c)
        return pltpu.make_async_remote_copy(
            src_ref=window.at[1 + c, rows], dst_ref=window.at[block, rows],
            send_sem=spread_ssem.at[half, n], recv_sem=spread_rsem.at[half, slot],
            device_id=targets[n], device_id_type=MESH,
        )

    for far_half_too in (0, 1):
        for n, (i, j) in enumerate(moves):
            if j == far_half_too:
                from_x, from_zh = wrap(x - i, NX), wrap(zh - j, 2)
                gather_copy(from_x, from_zh, x, zh, n, from_zh * NX + from_x).wait_recv()
        for n in range(3):
            spread_copy(wrap(zh + far_half_too, 2), n).start()

    pltpu.make_async_copy(far_half, far_half, acts_sems.at[0]).wait()
    vg_copy.wait_send()
    for flow in range(2 * KV_HEADS):
        for step in range(FLOWS[flow][2]):
            for sub in range(2):
                ring_copy(flow, step, sub).wait_send()
    for i in range(1, RING):
        zx_copy(wrap(z + i, NZ), z).wait_send()
        yx_copy(wrap(y + i, NY), y).wait_send()
    for i in range(1, NX):
        x_copy(wrap(x + i, NX), x).wait_send()
    for n, (i, j) in enumerate(moves):
        gather_copy(x, zh, wrap(x + i, NX), wrap(zh + j, 2), n, zh * NX + x).wait_send()

    def ordered(block):
        parts = [
            window[block, (h * NX + g) * HALF : (h * NX + g + 1) * HALF, :]
            for g in range(NX)
            for h in range(2)
        ]
        return jnp.concatenate(parts, axis=0)

    def picked(start, blocks):
        columns = jnp.concatenate([ordered(block) for block in blocks], axis=1)
        part = jnp.concatenate(
            [chosen_buf[pl.ds(start, PICK), pl.ds(block * BLOCK, BLOCK)] for block in blocks],
            axis=1,
        )
        return nt_dot(part, columns)

    def arrived(block, slot):
        for half in range(2):
            part = window.at[block, pl.ds(half * NX * HALF, NX * HALF)]
            pltpu.make_async_copy(part, part, spread_rsem.at[half, slot]).wait()

    starts = range(0, slot_ref.shape[0], PICK)
    arrived(2 - c, 2)
    for start in starts:
        slot_buf[pl.ds(start, PICK), :] = picked(start, (1, 2))
    arrived(3, 0)
    arrived(0, 1)
    for start in starts:
        rows = pl.ds(start, PICK)
        slot_ref[rows, :] = (slot_buf[rows, :] + picked(start, (0, 3))).astype(BF16)

    for half in range(2):
        for n in range(3):
            spread_copy(half, n).wait_send()


def shards(activations, queries, keys, values, out_grad, positions, shard_table):
    tokens, width = keys.shape
    stride = activations.shape[1] // lax.axis_size("fsdp")
    slot_rows = stride + stride // 4
    vmem = pl.BlockSpec(memory_space=pltpu.VMEM)
    hbm = pl.BlockSpec(memory_space=pltpu.HBM)
    dma = pltpu.SemaphoreType.DMA
    ring = (2 * KV_HEADS, HOPS, 2)
    key_grad, slot_grad = pl.pallas_call(
        kernel,
        out_shape=(
            pltpu.VMEM((tokens, width), BF16),
            pltpu.VMEM((slot_rows, width), BF16),
        ),
        in_specs=[pl.BlockSpec(memory_space=pltpu.SMEM), vmem] + [hbm] * 5,
        out_specs=(vmem, vmem),
        scratch_shapes=[
            pltpu.VMEM(queries.shape, BF16),
            pltpu.VMEM(keys.shape, BF16),
            pltpu.VMEM(values.shape, BF16),
            pltpu.VMEM(out_grad.shape, BF16),
            pltpu.VMEM((NY * NZL, 2 * BLOCK, BLOCK), BF16),
            pltpu.VMEM((width, 2 * BLOCK), BF16),
            pltpu.VMEM((KV_HEADS * GROUP // 2, BLOCK, 2 * BLOCK), F32),
            pltpu.VMEM(ring + (HALF, 4 * BLOCK), BF16),
            pltpu.VMEM(ring + (HALF, 4 * BLOCK), BF16),
            pltpu.VMEM((NZ, 2, HALF, BLOCK), BF16),
            pltpu.VMEM((NZ, 2, HALF, BLOCK), BF16),
            pltpu.VMEM((NY, 2, HALF, BLOCK), BF16),
            pltpu.VMEM((NY, 2, HALF, BLOCK), BF16),
            pltpu.VMEM((NX, HALF, BLOCK), BF16),
            pltpu.VMEM((NX, HALF, BLOCK), BF16),
            pltpu.VMEM((4, width, BLOCK), BF16),
            pltpu.VMEM((slot_rows, 4 * BLOCK), BF16),
            pltpu.VMEM((slot_rows, width), F32),
            dma((10,)), dma((1,)), dma((2,)), dma((2,)), dma(ring), dma(ring),
            dma((RING,)), dma((RING,)), dma((RING,)), dma((RING,)), dma((NX,)), dma((NX,)),
            dma((RING,)), dma((RING,)), dma((2, 3)), dma((2, 3)),
        ],
        compiler_params=pltpu.CompilerParams(
            collective_id=0, has_side_effects=True, vmem_limit_bytes=62 * 1024 * 1024
        ),
        cost_estimate=pl.CostEstimate(
            flops=2 * 10**9, bytes_accessed=6 * 2**20, transcendentals=2**19
        ),
    )(
        shard_table.reshape(1, 2), positions.reshape(1, tokens),
        queries, keys, values, out_grad, activations,
    )
    return (key_grad, slot_grad.reshape(1, 1, slot_rows, width))


def solution(mesh):
    return jax.shard_map(
        shards,
        mesh=mesh,
        in_specs=(
            P(("rep", "fsdp"), None),
            P(("rep", "fsdp"), None),
            P(("rep", "fsdp"), None),
            P(("rep", "fsdp"), None),
            P(("rep", "fsdp"), None),
            P(("rep", "fsdp")),
            P("rep", "fsdp", None),
        ),
        out_specs=(P(("rep", "fsdp"), None), P("rep", "fsdp", None, None)),
        check_vma=False,
    )
```
